128 devices in a mesh: seq: 8 (over x, core), exp: 16 (over z, y).
Axes of the slice: x: 4, y: 4, z: 4, core: 2. Of those that a mesh axis runs over, the one named last changes fastest.
Arguments:
- frames: bfloat16 [16, 1024, 1024], P('exp', 'seq'), may hold values from -6 to 6
- cotangent: bfloat16 [16, 1024, 1024], P('exp', 'seq'), may hold values from -3 to 3
- lengths: int32 [16], P('exp'), may hold values from 256 to 1024, as said below
- qkv_weight: bfloat16 [1024, 1536], replicated, may hold values from -1 to 1
- out_weight: bfloat16 [512, 1024], replicated, may hold values from -0.25 to 0.25
- router: float32 [128, 1024], P(('seq', 'exp')), may hold values from -0.1875 to 0.1875
- expert_in: bfloat16 [128, 1024, 2048], P(('seq', 'exp')), may hold values from -0.1875 to 0.1875
- expert_out: bfloat16 [128, 2048, 1024], P(('seq', 'exp')), may hold values from -0.125 to 0.125
- send_index: int32 [128, 128, 3], P(('seq', 'exp')), may hold values from 0 to 127, as said below
- send_count: int32 [128, 128], P(('seq', 'exp')), may hold values from 0 to 3, as said below
Outputs:
- output: bfloat16 [16, 1024, 1024], P('exp', 'seq')
- grad_resid: bfloat16 [16, 1024, 1024], P('exp', 'seq')
- grad_expert_in: bfloat16 [128, 1024, 2048], P(('seq', 'exp'))
- grad_expert_out: bfloat16 [128, 2048, 1024], P(('seq', 'exp'))
- grad_router: float32 [128, 1024], P(('seq', 'exp'))
The draws below stay inside these ranges and needn't reach their ends.
Inputs may be any that keep to these rules, and one draw needn't show every extreme that they name: For i < send_count[p, j], slot i of send_index[p, j] names a local frame of source p chosen by expert j; these are distinct within [p, j]. Later slots are unused. `send_count`: every column sums to 256, so each expert takes exactly 256 frames in all; every column has an entry equal to 3. `lengths`: some utterance has all 1024 frames live.
All inputs are finite; a program needn't handle non-finite values.
Results may differ from the reference program's by a relative error of at most 0.022.
Values may be sent and summed in bfloat16 or wider, within the bound.
No kernel may reach another device: no remote copies, remote signals or barrier semaphores. Data moves between devices by JAX's collectives and lax.ppermute only.
A program may use at most 128 MiB of HBM per device.

```python
import jax
import jax.numpy as jnp
from jax import lax

D = 1024
HEADS = 8
HD = 64
FF = 2048
FR_DEV = 128
LEN = 1024
UTTS = 16
EXPERTS = 128
SLOT = 3
N_SEQ = 8


def draw_lengths(key, part):
    key = jax.random.fold_in(key, 7)
    first, second = jax.random.split(key)
    drawn = jax.random.randint(first, (UTTS,), LEN // 4, LEN + 1, dtype=jnp.int32)
    longest = jax.random.randint(second, (), 0, UTTS, dtype=jnp.int32)
    return jnp.where(jnp.arange(UTTS, dtype=jnp.int32) == longest, LEN, drawn).astype(jnp.int32)


def draw_send_count(key, part):
    key = jax.random.fold_in(key, 5)
    first, second, third = jax.random.split(key, 3)
    spare = FR_DEV // EXPERTS
    middle = 2 * spare
    pairs = EXPERTS // 2
    offset = jax.random.randint(first, (pairs, EXPERTS), -spare, spare + 1, dtype=jnp.int32)
    fullest = jax.random.randint(second, (EXPERTS,), 0, pairs, dtype=jnp.int32)
    offset = jnp.where(jnp.arange(pairs, dtype=jnp.int32)[:, None] == fullest[None, :], spare, offset)
    counts = jnp.stack([middle + offset, middle - offset], axis=1).reshape(EXPERTS, EXPERTS)
    shuffle_keys = jax.random.randint(third, (EXPERTS, EXPERTS), 0, EXPERTS, dtype=jnp.int32)
    ranked = shuffle_keys * EXPERTS + jnp.arange(EXPERTS, dtype=jnp.int32)[:, None]
    order = jnp.argsort(ranked, axis=0)
    return jnp.take_along_axis(counts, order, axis=0).astype(jnp.int32)


def draw_send_index(key, part):
    key = jax.random.fold_in(key, 3)
    keyed = jax.random.randint(key, (EXPERTS, EXPERTS, FR_DEV), 0, FR_DEV, dtype=jnp.int32)
    scores = keyed * FR_DEV + jnp.arange(FR_DEV, dtype=jnp.int32)
    return lax.top_k(scores, SLOT)[1].astype(jnp.int32)


def draw_qkv_weight(key, part):
    key = jax.random.fold_in(key, 11)
    first, second, third = jax.random.split(key, 3)
    head_width = HEADS * HD
    query_part = jnp.clip(jax.random.normal(first, (D, head_width), jnp.float32), -6.0, 6.0) * D ** (-0.5)
    value_part = jnp.clip(jax.random.normal(third, (D, head_width), jnp.float32), -6.0, 6.0) * D ** (-0.5)
    key_part = jnp.clip(jax.random.normal(second, (D, head_width), jnp.float32), -6.0, 6.0) * D ** (-0.5)
    joined = jnp.concatenate([query_part, key_part, value_part], axis=1)
    return jnp.clip(joined, -1.0, 1.0).astype(jnp.bfloat16)


def block_levels(own_key, extent, shards, smallest, high):
    factor_of = 1.0
    for axis_at, parts in shards:
        draws = jax.random.uniform(jax.random.fold_in(jax.random.fold_in(own_key, 6), axis_at), (parts,), jnp.float32, smallest / len(shards), high / len(shards))
        factor_of = factor_of * jnp.repeat(jnp.exp(draws), extent[axis_at] // parts).reshape((-1,) + (1,) * (len(extent) - 1 - axis_at))
    return factor_of


def normal_values(own_key, shape, scale, limit, cuts=(), held_as=jnp.bfloat16):
    gain = block_levels(own_key, shape, cuts, -0.22, 0.18) if cuts else 1.0
    values = jax.random.normal(own_key, shape, jnp.float32) * scale * gain
    return jnp.minimum(jnp.maximum(values, -limit), limit).astype(held_as)


def setup_inputs(seed: int = 0) -> dict:
    streams_of = jax.random.split(jax.random.key(seed), 11)
    frames = normal_values(streams_of[0], (UTTS, LEN, D), 1.0, 6.0, ((0, 16), (1, 8)))
    cotangent = normal_values(streams_of[1], (UTTS, LEN, D), 0.5, 3.0, ((0, 16), (1, 8)))
    lengths = draw_lengths(jax.random.fold_in(streams_of[10], 71), 0)
    qkv_weight = draw_qkv_weight(jax.random.fold_in(streams_of[10], 71), 0)
    out_weight = normal_values(streams_of[4], (HEADS * HD, D), (HEADS * HD) ** -0.5, 0.25)
    router = normal_values(streams_of[5], (EXPERTS, D), D ** -0.5, 0.1875, ((0, 128),), jnp.float32)
    expert_in = normal_values(streams_of[6], (EXPERTS, D, FF), D ** -0.5, 0.1875, ((0, 128),))
    expert_out = normal_values(streams_of[7], (EXPERTS, FF, D), FF ** -0.5, 0.125, ((0, 128),))
    send_index = draw_send_index(jax.random.fold_in(streams_of[10], 71), 0)
    send_count = draw_send_count(jax.random.fold_in(streams_of[10], 71), 0)
    return dict(frames=frames, cotangent=cotangent, lengths=lengths, qkv_weight=qkv_weight, out_weight=out_weight, router=router, expert_in=expert_in, expert_out=expert_out, send_index=send_index, send_count=send_count)


epsilon = 1e-05
masked_score = -1e+30

def normalize(values):
    center = lax.optimization_barrier(jnp.mean(values, axis=-1, keepdims=True))
    spread = lax.optimization_barrier(jnp.mean(jnp.square(values - center), axis=-1, keepdims=True))
    return (values - center) * lax.rsqrt(spread + epsilon)

def norm_backward(values, upstream):
    center = lax.optimization_barrier(jnp.mean(values, axis=-1, keepdims=True))
    spread = lax.optimization_barrier(jnp.mean(jnp.square(values - center), axis=-1, keepdims=True))
    inverse = lax.rsqrt(spread + epsilon)
    unit_rows = (values - center) * inverse
    first_mean = lax.optimization_barrier(jnp.mean(upstream, axis=-1, keepdims=True))
    second_mean = lax.optimization_barrier(jnp.mean(upstream * unit_rows, axis=-1, keepdims=True))
    return inverse * (upstream - first_mean - unit_rows * second_mean)

def expert_forward(rows_x, w_first, w_second, router_row):
    logits = jnp.dot(rows_x.astype(jnp.float32), router_row, precision=lax.Precision.HIGHEST)
    gates = jax.nn.sigmoid(logits)
    before = jnp.dot(rows_x, w_first, preferred_element_type=jnp.float32)
    activated = jax.nn.gelu(before).astype(jnp.bfloat16)
    expert_rows = jnp.dot(activated, w_second, preferred_element_type=jnp.float32)
    returned = (gates[:, None] * expert_rows).astype(jnp.bfloat16)
    return (gates, before, activated, expert_rows, returned)

def expert_backward(rows_x, rows_g, w_first, w_second, router_row, saved):
    gates, before, activated, expert_rows = saved
    grads_wide = rows_g.astype(jnp.float32)
    out_grad = (gates[:, None] * grads_wide).astype(jnp.bfloat16)
    logit_grad = lax.optimization_barrier(jnp.sum(grads_wide * expert_rows, axis=1)) * gates * (1.0 - gates)
    act_grad = jnp.dot(out_grad, w_second.T, preferred_element_type=jnp.float32)
    _, gelu_pull = jax.vjp(jax.nn.gelu, before)
    before_grad = gelu_pull(act_grad)[0].astype(jnp.bfloat16)
    row_grad = jnp.dot(before_grad, w_first.T, preferred_element_type=jnp.float32)
    row_grad = (row_grad + logit_grad[:, None] * router_row[None, :]).astype(jnp.bfloat16)
    grad_second = jnp.dot(activated.T, out_grad, preferred_element_type=jnp.float32).astype(jnp.bfloat16)
    grad_first = jnp.dot(rows_x.T, before_grad, preferred_element_type=jnp.float32).astype(jnp.bfloat16)
    grad_route = jnp.dot(logit_grad, rows_x.astype(jnp.float32), precision=lax.Precision.HIGHEST)
    return (row_grad, grad_first, grad_second, grad_route)

def to_sources(array):
    return array.reshape(UTTS, N_SEQ, FR_DEV, D).transpose(1, 0, 2, 3).reshape(N_SEQ * UTTS, FR_DEV, D)

def from_sources(array):
    return array.reshape(N_SEQ, UTTS, FR_DEV, D).transpose(1, 0, 2, 3).reshape(UTTS, LEN, D)

def attend(item):
    queries, key_rows, value_rows, length = item
    score_scale = HD ** (-0.5)
    scores = jnp.einsum('qhd,khd->hqk', queries.astype(jnp.float32), key_rows.astype(jnp.float32)) * score_scale
    in_range = jnp.arange(LEN, dtype=jnp.int32) < length
    masked = jnp.where(in_range[None, None, :], scores, masked_score)
    row_top = lax.optimization_barrier(jnp.max(masked, axis=-1, keepdims=True))
    weights = jnp.where(in_range[None, None, :], jnp.exp(masked - row_top), 0.0)
    row_total = lax.optimization_barrier(jnp.sum(weights, axis=-1))
    probs = weights.astype(jnp.bfloat16)
    weighted = jnp.einsum('hqk,khd->qhd', probs.astype(jnp.float32), value_rows.astype(jnp.float32))
    return (weighted / row_total.T[:, :, None]).astype(jnp.bfloat16).reshape(LEN, HEADS * HD)

def reference(frames, cotangent, lengths, qkv_weight, out_weight, router, expert_in, expert_out, send_index, send_count):
    head_width = HEADS * HD
    normed = normalize(frames.astype(jnp.float32)).astype(jnp.bfloat16)
    projected = jnp.dot(normed.reshape(UTTS * LEN, D), qkv_weight, preferred_element_type=jnp.float32)
    projected = projected.astype(jnp.bfloat16).reshape(UTTS, LEN, 3, HEADS, HD)
    attended = lax.map(attend, (projected[:, :, 0], projected[:, :, 1], projected[:, :, 2], lengths))
    mixed = jnp.dot(attended.reshape(UTTS * LEN, head_width), out_weight, preferred_element_type=jnp.float32)
    resid = (frames.astype(jnp.float32) + mixed.reshape(UTTS, LEN, D)).astype(jnp.bfloat16)
    resid_wide = resid.astype(jnp.float32)
    mid_rows = normalize(resid_wide).astype(jnp.bfloat16)
    source_x = to_sources(mid_rows)
    source_g = to_sources(cotangent)
    slot_ids = jnp.arange(SLOT, dtype=jnp.int32)
    owners = jnp.arange(EXPERTS, dtype=jnp.int32)[:, None]
    blank = jnp.zeros((), jnp.bfloat16)

    def per_expert(carry, item):
        sum_out, sum_grad = carry
        chosen, counts, w_first, w_second, router_row = item
        in_use = (slot_ids[None, :] < counts[:, None])[:, :, None]
        rows_x = jnp.where(in_use, source_x[owners, chosen], blank).reshape(EXPERTS * SLOT, D)
        rows_g = jnp.where(in_use, source_g[owners, chosen], blank).reshape(EXPERTS * SLOT, D)
        gates, before, activated, expert_rows, returned = expert_forward(rows_x, w_first, w_second, router_row)
        row_grad, grad_first, grad_second, grad_route = expert_backward(rows_x, rows_g, w_first, w_second, router_row, (gates, before, activated, expert_rows))
        sum_out = sum_out.at[owners, chosen].add(returned.reshape(EXPERTS, SLOT, D).astype(jnp.float32))
        sum_grad = sum_grad.at[owners, chosen].add(row_grad.reshape(EXPERTS, SLOT, D).astype(jnp.float32))
        return ((sum_out, sum_grad), (grad_first, grad_second, grad_route))
    start = (jnp.zeros((EXPERTS, FR_DEV, D), jnp.float32), jnp.zeros((EXPERTS, FR_DEV, D), jnp.float32))
    items = (send_index.transpose(1, 0, 2), send_count.T, expert_in, expert_out, router)
    (sum_out, sum_grad), (grad_first, grad_second, grad_route) = lax.scan(per_expert, start, items)
    output = (resid_wide + from_sources(sum_out)).astype(jnp.bfloat16)
    grad_resid = (cotangent.astype(jnp.float32) + norm_backward(resid_wide, from_sources(sum_grad))).astype(jnp.bfloat16)
    return (output, grad_resid, grad_first, grad_second, grad_route)
```

```python
import jax
import jax.numpy as jnp
from jax import lax
from jax.experimental import pallas as pl
from jax.experimental.pallas import tpu as pltpu
from jax.sharding import PartitionSpec as P

HEADS = 8
HD = 64
D = 1024
FF = 2048
FR = 128
DEVS = 128
SLOT = 3
KEYS = 1024
LIVE = 256
TILES = D // 128
ROWS = SLOT * TILES
PAIR = 2 * HD

epsilon = 1e-05
masked_score = -1e30
empty_mark = 2.0**100
empty_bound = 2.0**99

F32 = jnp.float32
BF16 = jnp.bfloat16
MB = 1024 * 1024


def params(mib, semantics=None):
    return pltpu.CompilerParams(vmem_limit_bytes=mib * MB, dimension_semantics=semantics)


def whole(shape):
    return pl.BlockSpec(shape, lambda *_: (0,) * len(shape))


def dot(a, b, dims=((1,), (0,))):
    return lax.dot_general(a, b, (dims, ((), ())), preferred_element_type=F32)


def normalize(values):
    center = jnp.mean(values, axis=-1, keepdims=True)
    shifted = values - center
    spread = jnp.mean(jnp.square(shifted), axis=-1, keepdims=True)
    inverse = lax.rsqrt(spread + epsilon)
    return shifted * inverse, inverse


def spread_matrix(index_ref, count_ref, slot):
    frame = lax.broadcasted_iota(jnp.int32, (FR, DEVS), 0)
    named = jnp.broadcast_to(index_ref[slot : slot + 1, :], (FR, DEVS)) == frame
    used = jnp.broadcast_to(count_ref[...], (FR, DEVS)) > slot
    return jnp.where(named & used, 1.0, 0.0)


def pack_rows(stage, rows, per, first):
    for tile in range(TILES):
        stage[pl.ds(first + tile, DEVS, stride=per), :] = rows[:, tile * 128 : (tile + 1) * 128]


def unpack_rows(stage, per, first):
    return jnp.concatenate(
        [stage[pl.ds(first + tile, DEVS, stride=per), :] for tile in range(TILES)], axis=1
    )


def project_kernel(frames_ref, weight_ref, kv_ref, q_ref, normed):
    step = pl.program_id(0)

    @pl.when(step == 0)
    def _():
        normed[...] = normalize(frames_ref[...].astype(F32))[0].astype(BF16)

    block = dot(normed[...], weight_ref[...]).astype(BF16)

    @pl.when(step < 2)
    def _():
        kv_ref[...] = block

    @pl.when(step == 2)
    def _():
        q_ref[...] = block


def project(frames, weight):
    half = HEADS * HD
    return pl.pallas_call(
        project_kernel,
        grid=(3,),
        in_specs=[
            whole((FR, D)),
            pl.BlockSpec((D, half), lambda n: (0, lax.rem(n + 1, 3))),
        ],
        out_specs=[
            pl.BlockSpec((FR, half), lambda n: (0, jnp.minimum(n, 1))),
            whole((FR, half)),
        ],
        out_shape=[
            jax.ShapeDtypeStruct((FR, 2 * half), BF16),
            jax.ShapeDtypeStruct((FR, half), BF16),
        ],
        scratch_shapes=[pltpu.VMEM((FR, D), BF16)],
        compiler_params=params(32),
        cost_estimate=pl.CostEstimate(
            flops=2 * FR * D * 3 * half, bytes_accessed=4 * MB, transcendentals=0
        ),
    )(frames, weight)


def gather_kernel(table_ref, index_ref, count_ref, out_ref, stage):
    count_column = jnp.broadcast_to(count_ref[...].astype(F32), (DEVS, DEVS)).T
    for slot in range(SLOT):
        pick = spread_matrix(index_ref, count_ref, slot).T.astype(BF16)
        rows = dot(pick, table_ref[...])
        mark = jnp.where(count_column[:, 0:1] > slot, 0.0, empty_mark)
        pack_rows(stage, rows + mark, ROWS, slot * TILES)
    out_ref[...] = stage[...].astype(BF16)


def gather_rows(table, index, count):
    return pl.pallas_call(
        gather_kernel,
        out_shape=jax.ShapeDtypeStruct((DEVS * ROWS, 128), BF16),
        scratch_shapes=[pltpu.VMEM((DEVS * ROWS, 128), F32)],
        compiler_params=params(32),
        cost_estimate=pl.CostEstimate(
            flops=2 * DEVS * SLOT * FR * D, bytes_accessed=2 * MB, transcendentals=0
        ),
    )(table, index, count)


def attend_kernel(
    length_ref, q_ref, k_ref, v_ref, frames_ref, weight_ref, index_ref, count_ref,
    resid_ref, rows_ref, attended, stage,
):
    step = pl.program_id(0)
    low = lax.broadcasted_iota(jnp.int32, (FR, PAIR), 1) < HD
    q = q_ref[...].astype(F32) * HD ** (-0.5)
    both = jnp.concatenate([jnp.where(low, q, 0.0), jnp.where(low, 0.0, q)], axis=0).astype(BF16)
    scores = dot(both, k_ref[...], ((1,), (1,)))
    live = lax.broadcasted_iota(jnp.int32, (1, KEYS), 1) < length_ref[0]
    scores = jnp.where(live, scores, masked_score)
    top = jnp.max(scores, axis=-1, keepdims=True)
    weights = jnp.exp(scores - top)
    total = jnp.sum(weights, axis=-1, keepdims=True)
    mixed = dot(weights.astype(BF16), v_ref[...]) / total
    attended[:, pl.ds(pl.multiple_of(step * PAIR, PAIR), PAIR)] = jnp.where(
        low, mixed[:FR], mixed[FR:]
    ).astype(BF16)

    @pl.when(step == HEADS // 2 - 1)
    def _():
        resid = (frames_ref[...].astype(F32) + dot(attended[...], weight_ref[...])).astype(BF16)
        resid_ref[...] = resid
        mid = normalize(resid.astype(F32))[0].astype(BF16)
        for slot in range(SLOT):
            pick = spread_matrix(index_ref, count_ref, slot).T.astype(BF16)
            pack_rows(stage, dot(pick, mid), ROWS, slot * TILES)
        rows_ref[...] = stage[...].astype(BF16)


def attend(length, q, kv, frames, weight, index, count):
    pairs = HEADS // 2
    return pl.pallas_call(
        attend_kernel,
        grid_spec=pltpu.PrefetchScalarGridSpec(
            num_scalar_prefetch=1,
            grid=(pairs,),
            in_specs=[
                pl.BlockSpec((FR, PAIR), lambda n, _: (0, n)),
                pl.BlockSpec((KEYS, PAIR), lambda n, _: (0, n)),
                pl.BlockSpec((KEYS, PAIR), lambda n, _: (0, n + pairs)),
                whole((FR, D)),
                whole((HEADS * HD, D)),
                whole((SLOT, DEVS)),
                whole((1, DEVS)),
            ],
            out_specs=[whole((FR, D)), whole((DEVS * ROWS, 128))],
            scratch_shapes=[
                pltpu.VMEM((FR, HEADS * HD), BF16),
                pltpu.VMEM((DEVS * ROWS, 128), F32),
            ],
        ),
        out_shape=[
            jax.ShapeDtypeStruct((FR, D), BF16),
            jax.ShapeDtypeStruct((DEVS * ROWS, 128), BF16),
        ],
        compiler_params=params(40),
        cost_estimate=pl.CostEstimate(
            flops=8 * FR * KEYS * HEADS * HD, bytes_accessed=5 * MB,
            transcendentals=FR * KEYS * HEADS,
        ),
    )(length, q, kv, kv, frames, weight, index, count)


FF_TILE = 512


def prepare_kernel(rows_ref, second_ref, grads_ref, place_ref, take_ref, pulled_ref, stage):
    @pl.when(pl.program_id(0) == 0)
    def _():
        stage[...] = rows_ref[...].astype(F32)
        rows = [unpack_rows(stage, ROWS, slot * TILES) for slot in range(SLOT)]
        rows = jnp.concatenate(rows, axis=0)
        total = SLOT * DEVS
        live = rows[:, 0:128] < empty_bound
        before = lax.broadcasted_iota(jnp.int32, (total, total), 0) >= lax.broadcasted_iota(
            jnp.int32, (total, total), 1
        )
        ranks = dot(
            jnp.where(before, 1.0, 0.0).astype(BF16), jnp.where(live, 1.0, 0.0).astype(BF16)
        )
        seat = jnp.where(live, ranks - 1.0, -1.0)[:, 0:1].astype(jnp.int32)
        place = jnp.where(
            seat == lax.broadcasted_iota(jnp.int32, (total, LIVE), 1), 1.0, 0.0
        )
        take = place.T.astype(BF16)
        place_ref[...] = place.astype(BF16)
        take_ref[...] = take
        grads_ref[...] = dot(take, rows.astype(BF16)).astype(BF16)

    pulled_ref[...] = dot(grads_ref[...], second_ref[...], ((1,), (1,)))


def prepare(rows, second):
    total = SLOT * DEVS
    return pl.pallas_call(
        prepare_kernel,
        grid=(FF // FF_TILE,),
        in_specs=[whole((DEVS * ROWS, 128)), pl.BlockSpec((FF_TILE, D), lambda n: (n, 0))],
        out_specs=[
            whole((LIVE, D)),
            whole((total, LIVE)),
            whole((LIVE, total)),
            pl.BlockSpec((LIVE, FF_TILE), lambda n: (0, n)),
        ],
        out_shape=[
            jax.ShapeDtypeStruct((LIVE, D), BF16),
            jax.ShapeDtypeStruct((total, LIVE), BF16),
            jax.ShapeDtypeStruct((LIVE, total), BF16),
            jax.ShapeDtypeStruct((LIVE, FF), F32),
        ],
        scratch_shapes=[pltpu.VMEM((DEVS * ROWS, 128), F32)],
        compiler_params=params(32),
        cost_estimate=pl.CostEstimate(
            flops=2 * LIVE * D * FF, bytes_accessed=8 * MB, transcendentals=0
        ),
    )(rows, second)


gelu_scale = (2.0 / jnp.pi) ** 0.5
gelu_cubic = 0.044715


def expert_kernel(
    rows_ref, take_ref, place_ref, grads_ref, pulled_ref, first_ref, second_ref, router_ref,
    back_ref, picked_ref, active_ref, before_grad_ref, out_grad_ref, route_grad_ref,
    stage, gates, result, row_grad, logit,
):
    step = pl.program_id(0)
    steps = pl.num_programs(0)

    @pl.when(step == 0)
    def _():
        stage[pl.ds(0, DEVS * ROWS), :] = rows_ref[...].astype(F32)
        rows = [
            unpack_rows(stage, ROWS, slot * TILES).astype(BF16) for slot in range(SLOT)
        ]
        picked = dot(take_ref[...], jnp.concatenate(rows, axis=0))
        picked_ref[...] = picked.astype(BF16)
        logits = jnp.sum(picked * router_ref[...], axis=-1, keepdims=True)
        gate = 1.0 / (1.0 + jnp.exp(-logits))
        gates[...] = jnp.broadcast_to(gate, gates.shape)
        out_grad_ref[...] = (gate * grads_ref[...].astype(F32)).astype(BF16)
        result[...] = jnp.zeros_like(result)
        row_grad[...] = jnp.zeros_like(row_grad)
        logit[...] = jnp.zeros_like(logit)

    first = first_ref[...]
    before = dot(picked_ref[...], first)
    square = before * before
    bend = jnp.tanh(gelu_scale * before * (1.0 + gelu_cubic * square))
    half = 0.5 * (1.0 + bend)
    active = (before * half).astype(BF16)
    slope = half + 0.5 * before * (1.0 - bend * bend) * (
        gelu_scale * (1.0 + 3.0 * gelu_cubic * square)
    )
    pulled = pulled_ref[...]
    gate = gates[:, 0:1]
    before_grad = (gate * pulled * slope).astype(BF16)
    active_ref[...] = active
    before_grad_ref[...] = before_grad
    logit[...] += jnp.sum(active.astype(F32) * pulled, axis=-1, keepdims=True)
    result[...] += dot(active, second_ref[...])
    row_grad[...] += dot(before_grad, first, ((1,), (1,)))

    @pl.when(step == steps - 1)
    def _():
        gate = gates[:, 0:1]
        logit_grad = logit[:, 0:1] * gate * (1.0 - gate)
        route_grad_ref[...] = jnp.sum(
            logit_grad * picked_ref[...].astype(F32), axis=0, keepdims=True
        )
        returned = (gate * result[...]).astype(BF16)
        back = (row_grad[...] + logit_grad * router_ref[...]).astype(BF16)
        for slot in range(SLOT):
            place = place_ref[pl.ds(slot * DEVS, DEVS), :]
            pack_rows(stage, dot(place, returned), 2 * ROWS, slot * TILES)
            pack_rows(stage, dot(place, back), 2 * ROWS, ROWS + slot * TILES)
        back_ref[...] = stage[...].astype(BF16)


def expert(rows, take, place, grads, pulled, first, second, router):
    total = SLOT * DEVS
    tile = FF_TILE
    return pl.pallas_call(
        expert_kernel,
        grid=(FF // tile,),
        in_specs=[
            whole((DEVS * ROWS, 128)),
            whole((LIVE, total)),
            whole((total, LIVE)),
            whole((LIVE, D)),
            pl.BlockSpec((LIVE, tile), lambda n: (0, n)),
            pl.BlockSpec((D, tile), lambda n: (0, n)),
            pl.BlockSpec((tile, D), lambda n: (n, 0)),
            whole((1, D)),
        ],
        out_specs=[
            whole((DEVS * ROWS * 2, 128)),
            whole((LIVE, D)),
            pl.BlockSpec((LIVE, tile), lambda n: (0, n)),
            pl.BlockSpec((LIVE, tile), lambda n: (0, n)),
            whole((LIVE, D)),
            whole((1, D)),
        ],
        out_shape=[
            jax.ShapeDtypeStruct((DEVS * ROWS * 2, 128), BF16),
            jax.ShapeDtypeStruct((LIVE, D), BF16),
            jax.ShapeDtypeStruct((LIVE, FF), BF16),
            jax.ShapeDtypeStruct((LIVE, FF), BF16),
            jax.ShapeDtypeStruct((LIVE, D), BF16),
            jax.ShapeDtypeStruct((1, D), F32),
        ],
        scratch_shapes=[
            pltpu.VMEM((DEVS * ROWS * 2, 128), F32),
            pltpu.VMEM((LIVE, 128), F32),
            pltpu.VMEM((LIVE, D), F32),
            pltpu.VMEM((LIVE, D), F32),
            pltpu.VMEM((LIVE, 128), F32),
        ],
        compiler_params=params(48),
        cost_estimate=pl.CostEstimate(
            flops=6 * LIVE * D * FF, bytes_accessed=14 * MB, transcendentals=LIVE * FF
        ),
    )(rows, take, place, grads, pulled, first, second, router)


def weight_grad_kernel(picked_ref, before_grad_ref, active_ref, out_grad_ref, first_ref, second_ref):
    first_ref[...] = dot(picked_ref[...], before_grad_ref[...], ((0,), (0,))).astype(BF16)
    second_ref[...] = dot(active_ref[...], out_grad_ref[...], ((0,), (0,))).astype(BF16)


def weight_grads(picked, before_grad, active, out_grad):
    tile = FF_TILE
    return pl.pallas_call(
        weight_grad_kernel,
        grid=(FF // tile,),
        in_specs=[
            whole((LIVE, D)),
            pl.BlockSpec((LIVE, tile), lambda n: (0, n)),
            pl.BlockSpec((LIVE, tile), lambda n: (0, n)),
            whole((LIVE, D)),
        ],
        out_specs=[
            pl.BlockSpec((D, tile), lambda n: (0, n)),
            pl.BlockSpec((tile, D), lambda n: (n, 0)),
        ],
        out_shape=[
            jax.ShapeDtypeStruct((D, FF), BF16),
            jax.ShapeDtypeStruct((FF, D), BF16),
        ],
        compiler_params=params(32),
        cost_estimate=pl.CostEstimate(
            flops=4 * LIVE * D * FF, bytes_accessed=11 * MB, transcendentals=0
        ),
    )(picked, before_grad, active, out_grad)


def combine_kernel(
    rows_ref, index_ref, count_ref, resid_ref, upstream_ref, output_ref, grad_ref, stage
):
    stage[...] = rows_ref[...].astype(F32)
    mixture = jnp.zeros((FR, D), F32)
    normed_grad = jnp.zeros((FR, D), F32)
    for slot in range(SLOT):
        spread = spread_matrix(index_ref, count_ref, slot).astype(BF16)
        rows = unpack_rows(stage, 2 * ROWS, slot * TILES).astype(BF16)
        mixture += dot(spread, rows)
        rows = unpack_rows(stage, 2 * ROWS, ROWS + slot * TILES).astype(BF16)
        normed_grad += dot(spread, rows)
    resid = resid_ref[...].astype(F32)
    output_ref[...] = (resid + mixture).astype(BF16)
    unit, inverse = normalize(resid)
    first_mean = jnp.mean(normed_grad, axis=-1, keepdims=True)
    second_mean = jnp.mean(normed_grad * unit, axis=-1, keepdims=True)
    grad = inverse * (normed_grad - first_mean - unit * second_mean)
    grad_ref[...] = (upstream_ref[...].astype(F32) + grad).astype(BF16)


def combine(rows, index, count, resid, upstream):
    return pl.pallas_call(
        combine_kernel,
        out_shape=[jax.ShapeDtypeStruct((FR, D), BF16)] * 2,
        scratch_shapes=[pltpu.VMEM((DEVS * ROWS * 2, 128), F32)],
        compiler_params=params(32),
        cost_estimate=pl.CostEstimate(
            flops=4 * DEVS * SLOT * FR * D, bytes_accessed=3 * MB, transcendentals=0
        ),
    )(rows, index, count, resid, upstream)


def deliver(rows, per):
    moved = lax.all_to_all(
        rows.reshape(DEVS, per, 128), ("seq", "exp"), split_axis=0, concat_axis=0, tiled=True
    )
    return moved.reshape(DEVS * per, 128)


def local(
    frames,
    cotangent,
    lengths,
    qkv_weight,
    out_weight,
    router,
    expert_in,
    expert_out,
    send_index,
    send_count,
):
    own_frames = frames[0]
    upstream = cotangent[0]
    first = expert_in[0]
    second = expert_out[0]
    index = send_index[0].T

    kv, q = project(own_frames, qkv_weight)
    all_kv = lax.all_gather(kv, "seq", axis=0, tiled=True)
    arrived_g = deliver(gather_rows(upstream, index, send_count), ROWS)
    resid, rows_x = attend(lengths, q, all_kv, own_frames, out_weight, index, send_count)
    arrived_x = deliver(rows_x, ROWS)
    grads, place, take, pulled = prepare(arrived_g, second)
    back, picked, active, before_grad, out_grad, grad_route = expert(
        arrived_x, take, place, grads, pulled, first, second, router
    )
    arrived_back = deliver(back, 2 * ROWS)
    grad_first, grad_second = weight_grads(picked, before_grad, active, out_grad)
    output, grad_resid = combine(arrived_back, index, send_count, resid, upstream)
    return (output[None], grad_resid[None], grad_first[None], grad_second[None], grad_route)


def solution(mesh):
    in_specs = (
        P("exp", "seq", None),
        P("exp", "seq", None),
        P("exp"),
        P(),
        P(),
        P(("seq", "exp"), None),
        P(("seq", "exp"), None, None),
        P(("seq", "exp"), None, None),
        P(("seq", "exp"), None, None),
        P(("seq", "exp"), None),
    )
    out_specs = (
        P("exp", "seq", None),
        P("exp", "seq", None),
        P(("seq", "exp"), None, None),
        P(("seq", "exp"), None, None),
        P(("seq", "exp"), None),
    )
    return jax.shard_map(local, mesh=mesh, in_specs=in_specs, out_specs=out_specs, check_vma=False)
```

```python
import jax
import jax.numpy as jnp
from jax import lax
from jax.experimental import pallas as pl
from jax.experimental.pallas import tpu as pltpu
from jax.sharding import PartitionSpec as P

HEADS = 8
HD = 64
D = 1024
FF = 2048
FR = 128
DEVS = 128
SLOT = 3
KEYS = 1024
LIVE = 256
TILES = D // 128
ROWS = SLOT * TILES

epsilon = 1e-05
masked_score = -1e30
empty_mark = 2.0**100
empty_bound = 2.0**99

F32 = jnp.float32
BF16 = jnp.bfloat16
MB = 1024 * 1024


def params(mib):
    return pltpu.CompilerParams(vmem_limit_bytes=mib * MB)


def whole(shape):
    return pl.BlockSpec(shape, lambda *_: (0,) * len(shape))


def dot(a, b, dims=((1,), (0,))):
    return lax.dot_general(a, b, (dims, ((), ())), preferred_element_type=F32)


def normalize(values):
    center = jnp.mean(values, axis=-1, keepdims=True)
    shifted = values - center
    spread = jnp.mean(jnp.square(shifted), axis=-1, keepdims=True)
    inverse = lax.rsqrt(spread + epsilon)
    return shifted * inverse, inverse


def spread_matrix(index_ref, count_ref, slot):
    frame = lax.broadcasted_iota(jnp.int32, (FR, DEVS), 0)
    named = jnp.broadcast_to(index_ref[slot : slot + 1, :], (FR, DEVS)) == frame
    used = jnp.broadcast_to(count_ref[...], (FR, DEVS)) > slot
    return jnp.where(named & used, 1.0, 0.0)


def pack_rows(stage, rows, per, first):
    for tile in range(TILES):
        stage[pl.ds(first + tile, DEVS, stride=per), :] = rows[:, tile * 128 : (tile + 1) * 128]


def unpack_rows(stage, per, first):
    return jnp.concatenate(
        [stage[pl.ds(first + tile, DEVS, stride=per), :] for tile in range(TILES)], axis=1
    )


PART = HD * 3
HALF = HEADS * HD


def project_kernel(frames_ref, weight_ref, out_ref, normed):
    step = pl.program_id(0)

    @pl.when(step == 0)
    def _():
        normed[...] = normalize(frames_ref[...].astype(F32))[0].astype(BF16)

    block = dot(normed[...], weight_ref[...]).T.astype(BF16)
    for head in range(HEADS):
        start = pl.multiple_of(head * PART + step * HD, HD)
        out_ref[pl.ds(start, HD), :] = block[head * HD : (head + 1) * HD]


def project(frames, weight):
    return pl.pallas_call(
        project_kernel,
        grid=(3,),
        in_specs=[whole((FR, D)), pl.BlockSpec((D, HALF), lambda n: (0, n))],
        out_specs=whole((HEADS * PART, FR)),
        out_shape=jax.ShapeDtypeStruct((HEADS * PART, FR), BF16),
        scratch_shapes=[pltpu.VMEM((FR, D), BF16)],
        compiler_params=params(56),
        cost_estimate=pl.CostEstimate(
            flops=2 * FR * D * 3 * HALF, bytes_accessed=4 * MB, transcendentals=0
        ),
    )(frames, weight)


def staged(stage):
    return stage[...].reshape(DEVS, 1, ROWS, 128).astype(BF16)


def gather_kernel(table_ref, index_ref, count_ref, out_ref, stage):
    count_column = jnp.broadcast_to(count_ref[...].astype(F32), (DEVS, DEVS)).T
    for slot in range(SLOT):
        pick = spread_matrix(index_ref, count_ref, slot).T.astype(BF16)
        rows = dot(pick, table_ref[...])
        mark = jnp.where(count_column[:, 0:1] > slot, 0.0, empty_mark)
        pack_rows(stage, rows + mark, ROWS, slot * TILES)
    out_ref[...] = staged(stage)


def gather_rows(table, index, count):
    return pl.pallas_call(
        gather_kernel,
        grid=(1,),
        in_specs=[whole((FR, D)), whole((SLOT, DEVS)), whole((1, DEVS))],
        out_specs=pl.BlockSpec((DEVS, 1, ROWS, 128), lambda n: (0, 1, 0, 0)),
        out_shape=jax.ShapeDtypeStruct((DEVS, 2, ROWS, 128), BF16),
        scratch_shapes=[pltpu.VMEM((DEVS * ROWS, 128), F32)],
        compiler_params=params(20),
        cost_estimate=pl.CostEstimate(
            flops=2 * DEVS * SLOT * FR * D, bytes_accessed=2 * MB, transcendentals=0
        ),
    )(table, index, count)


QUERIES = 256


def attend_kernel(length_ref, parts_ref, out_ref):
    parts = [parts_ref[s * PART : (s + 1) * PART, :] for s in range(HEADS)]
    q = jnp.concatenate([part[:HD] for part in parts], axis=1)
    k = jnp.concatenate([part[HD : 2 * HD] for part in parts], axis=1).astype(F32)
    k = (k * HD ** (-0.5)).T.astype(BF16)
    v = jnp.concatenate([part[2 * HD :] for part in parts], axis=1)
    live = lax.broadcasted_iota(jnp.int32, (KEYS, QUERIES), 0) < length_ref[0]
    for first in range(0, KEYS, QUERIES):
        scores = dot(k, q[:, first : first + QUERIES])
        scores = jnp.where(live, scores, masked_score)
        top = jnp.max(scores, axis=0, keepdims=True)
        weights = jnp.exp(scores - top)
        total = jnp.sum(weights, axis=0, keepdims=True)
        mixed = (dot(v, weights.astype(BF16)) / total).astype(BF16)
        for piece in range(QUERIES // FR):
            source = first // FR + piece
            out_ref[source * HD : (source + 1) * HD, :] = mixed[:, piece * FR : (piece + 1) * FR]


def attend(length, parts):
    return pl.pallas_call(
        attend_kernel,
        in_specs=[
            pl.BlockSpec(memory_space=pltpu.SMEM),
            pl.BlockSpec(memory_space=pltpu.VMEM),
        ],
        out_shape=jax.ShapeDtypeStruct((HALF, FR), BF16),
        compiler_params=params(24),
        cost_estimate=pl.CostEstimate(
            flops=4 * KEYS * KEYS * HD, bytes_accessed=MB // 2, transcendentals=KEYS * KEYS
        ),
    )(length, parts)


def residual_kernel(
    attended_ref, frames_ref, weight_ref, index_ref, count_ref, packed_ref,
    resid_ref, out_ref, stage,
):
    attended = attended_ref[...].astype(F32).T.astype(BF16)
    resid = (frames_ref[...].astype(F32) + dot(attended, weight_ref[...])).astype(BF16)
    resid_ref[...] = resid
    mid = normalize(resid.astype(F32))[0].astype(BF16)
    for slot in range(SLOT):
        pick = spread_matrix(index_ref, count_ref, slot).T.astype(BF16)
        pack_rows(stage, dot(pick, mid), ROWS, slot * TILES)
    out_ref[...] = staged(stage)


def residual(attended, frames, weight, index, count, packed):
    return pl.pallas_call(
        residual_kernel,
        grid=(1,),
        in_specs=[
            whole((HALF, FR)),
            whole((FR, D)),
            whole((HALF, D)),
            whole((SLOT, DEVS)),
            whole((1, DEVS)),
            pl.BlockSpec(memory_space=pl.ANY),
        ],
        out_specs=[
            whole((FR, D)),
            pl.BlockSpec((DEVS, 1, ROWS, 128), lambda n: (0, 0, 0, 0)),
        ],
        out_shape=[
            jax.ShapeDtypeStruct((FR, D), BF16),
            jax.ShapeDtypeStruct((DEVS, 2, ROWS, 128), BF16),
        ],
        input_output_aliases={5: 1},
        scratch_shapes=[pltpu.VMEM((DEVS * ROWS, 128), F32)],
        compiler_params=params(24),
        cost_estimate=pl.CostEstimate(
            flops=2 * FR * HALF * D + 2 * DEVS * SLOT * FR * D,
            bytes_accessed=3 * MB, transcendentals=0,
        ),
    )(attended, frames, weight, index, count, packed)


FF_TILE = 512
D_TILE = 256
FF_STEPS = FF // FF_TILE
gelu_scale = (2.0 / jnp.pi) ** 0.5
gelu_cubic = 0.044715


def seats(first_column):
    total = SLOT * DEVS
    live = first_column < empty_bound
    ahead = lax.broadcasted_iota(jnp.int32, (total, total), 0) >= lax.broadcasted_iota(
        jnp.int32, (total, total), 1
    )
    ranks = dot(jnp.where(ahead, 1.0, 0.0).astype(BF16), jnp.where(live, 1.0, 0.0).astype(BF16))
    seat = jnp.where(live, ranks - 1.0, -1.0)[:, 0:1].astype(jnp.int32)
    return jnp.where(seat == lax.broadcasted_iota(jnp.int32, (total, LIVE), 1), 1.0, 0.0)


def expert_kernel(
    rows_ref, first_hbm, second_hbm, router_ref,
    back_ref, picked_ref, active_ref, before_grad_ref, out_grad_ref, route_grad_ref,
    stage, first_ref, second_ref, first_sem, second_sem,
):
    loads = []
    for step in range(FF_STEPS):
        columns = pl.ds(step * FF_TILE, FF_TILE)
        loads.append((
            pltpu.make_async_copy(
                first_hbm.at[:, columns], first_ref.at[:, columns], first_sem.at[step]
            ),
            pltpu.make_async_copy(
                second_hbm.at[columns, :], second_ref.at[columns, :], second_sem.at[step]
            ),
        ))
    for pair in loads:
        for load in pair:
            load.start()

    stage[...] = rows_ref[...].astype(F32).reshape(DEVS * 2 * ROWS, 128)
    grads = [unpack_rows(stage, 2 * ROWS, ROWS + slot * TILES) for slot in range(SLOT)]
    grads = jnp.concatenate(grads, axis=0)
    place = seats(grads[:, 0:128])
    take = place.T.astype(BF16)
    place = place.astype(BF16)
    grads = dot(take, grads.astype(BF16)).astype(BF16)
    rows = [unpack_rows(stage, 2 * ROWS, slot * TILES).astype(BF16) for slot in range(SLOT)]
    picked_wide = dot(take, jnp.concatenate(rows, axis=0))
    picked = picked_wide.astype(BF16)
    picked_ref[...] = picked
    logits = jnp.sum(picked_wide * router_ref[...], axis=-1, keepdims=True)
    gate = 1.0 / (1.0 + jnp.exp(-logits))
    out_grad_ref[...] = (gate * grads.astype(F32)).astype(BF16)

    logit = jnp.zeros((LIVE, 1), F32)
    for step in range(FF_STEPS):
        columns = pl.ds(step * FF_TILE, FF_TILE)
        loads[step][0].wait()
        before = dot(picked, first_ref[:, columns])
        loads[step][1].wait()
        pulled = dot(grads, second_ref[columns, :], ((1,), (1,)))
        square = before * before
        bend = jnp.tanh(before * (gelu_scale + (gelu_scale * gelu_cubic) * square))
        half = 0.5 + 0.5 * bend
        active = (before * half).astype(BF16)
        slope = half + (before * (1.0 - bend * bend)) * (
            0.5 * gelu_scale + (1.5 * gelu_scale * gelu_cubic) * square
        )
        active_ref[:, columns] = active
        before_grad_ref[:, columns] = (gate * pulled * slope).astype(BF16)
        logit += jnp.sum(active.astype(F32) * pulled, axis=-1, keepdims=True)

    logit_grad = logit * gate * (1.0 - gate)
    route_grad_ref[...] = jnp.sum(logit_grad * picked_ref[...].astype(F32), axis=0, keepdims=True)
    for start in range(0, D, D_TILE):
        columns = pl.ds(start, D_TILE)
        result = dot(active_ref[...], second_ref[:, columns])
        returned = dot(place, (gate * result).astype(BF16))
        row_grad = dot(before_grad_ref[...], first_ref[columns, :], ((1,), (1,)))
        row_grad = row_grad + logit_grad * router_ref[:, columns]
        row_grad = dot(place, row_grad.astype(BF16))
        for slot in range(SLOT):
            sources = slice(slot * DEVS, (slot + 1) * DEVS)
            for tile in range(D_TILE // 128):
                lanes = slice(tile * 128, (tile + 1) * 128)
                at = slot * TILES + start // 128 + tile
                stage[pl.ds(at, DEVS, stride=2 * ROWS), :] = returned[sources, lanes]
                stage[pl.ds(ROWS + at, DEVS, stride=2 * ROWS), :] = row_grad[sources, lanes]
    back_ref[...] = stage[...].reshape(DEVS, 2, ROWS, 128).astype(BF16)


def expert(rows, first, second, router):
    vmem = pl.BlockSpec(memory_space=pltpu.VMEM)
    hbm = pl.BlockSpec(memory_space=pl.ANY)
    return pl.pallas_call(
        expert_kernel,
        in_specs=[vmem, hbm, hbm, vmem],
        out_specs=[vmem] * 6,
        out_shape=[
            jax.ShapeDtypeStruct((DEVS, 2, ROWS, 128), BF16),
            jax.ShapeDtypeStruct((LIVE, D), BF16),
            jax.ShapeDtypeStruct((LIVE, FF), BF16),
            jax.ShapeDtypeStruct((LIVE, FF), BF16),
            jax.ShapeDtypeStruct((LIVE, D), BF16),
            jax.ShapeDtypeStruct((1, D), F32),
        ],
        scratch_shapes=[
            pltpu.VMEM((DEVS * ROWS * 2, 128), F32),
            pltpu.VMEM((D, FF), BF16),
            pltpu.VMEM((FF, D), BF16),
            pltpu.SemaphoreType.DMA((FF_STEPS,)),
            pltpu.SemaphoreType.DMA((FF_STEPS,)),
        ],
        compiler_params=params(56),
        cost_estimate=pl.CostEstimate(
            flops=8 * LIVE * D * FF, bytes_accessed=14 * MB, transcendentals=LIVE * FF
        ),
    )(rows, first, second, router)


def weight_grad_kernel(picked_ref, before_grad_ref, active_ref, out_grad_ref, first_ref, second_ref):
    first_ref[...] = dot(picked_ref[...], before_grad_ref[...], ((0,), (0,))).astype(BF16)
    second_ref[...] = dot(active_ref[...], out_grad_ref[...], ((0,), (0,))).astype(BF16)


def weight_grads(picked, before_grad, active, out_grad):
    tile = FF_TILE
    return pl.pallas_call(
        weight_grad_kernel,
        grid=(FF // tile,),
        in_specs=[
            whole((LIVE, D)),
            pl.BlockSpec((LIVE, tile), lambda n: (0, n)),
            pl.BlockSpec((LIVE, tile), lambda n: (0, n)),
            whole((LIVE, D)),
        ],
        out_specs=[
            pl.BlockSpec((D, tile), lambda n: (0, n)),
            pl.BlockSpec((tile, D), lambda n: (n, 0)),
        ],
        out_shape=[
            jax.ShapeDtypeStruct((D, FF), BF16),
            jax.ShapeDtypeStruct((FF, D), BF16),
        ],
        compiler_params=params(24),
        cost_estimate=pl.CostEstimate(
            flops=4 * LIVE * D * FF, bytes_accessed=11 * MB, transcendentals=0
        ),
    )(picked, before_grad, active, out_grad)


def combine_kernel(
    rows_ref, index_ref, count_ref, resid_ref, upstream_ref, output_ref, grad_ref, stage
):
    stage[...] = rows_ref[...].astype(F32).reshape(DEVS * 2 * ROWS, 128)
    mixture = jnp.zeros((FR, D), F32)
    normed_grad = jnp.zeros((FR, D), F32)
    for slot in range(SLOT):
        spread = spread_matrix(index_ref, count_ref, slot).astype(BF16)
        rows = unpack_rows(stage, 2 * ROWS, slot * TILES).astype(BF16)
        mixture += dot(spread, rows)
        rows = unpack_rows(stage, 2 * ROWS, ROWS + slot * TILES).astype(BF16)
        normed_grad += dot(spread, rows)
    resid = resid_ref[...].astype(F32)
    output_ref[...] = (resid + mixture).astype(BF16)
    unit, inverse = normalize(resid)
    first_mean = jnp.mean(normed_grad, axis=-1, keepdims=True)
    second_mean = jnp.mean(normed_grad * unit, axis=-1, keepdims=True)
    grad = inverse * (normed_grad - first_mean - unit * second_mean)
    grad_ref[...] = (upstream_ref[...].astype(F32) + grad).astype(BF16)


def combine(rows, index, count, resid, upstream):
    return pl.pallas_call(
        combine_kernel,
        out_shape=[jax.ShapeDtypeStruct((FR, D), BF16)] * 2,
        scratch_shapes=[pltpu.VMEM((DEVS * ROWS * 2, 128), F32)],
        compiler_params=params(28),
        cost_estimate=pl.CostEstimate(
            flops=4 * DEVS * SLOT * FR * D, bytes_accessed=3 * MB, transcendentals=0
        ),
    )(rows, index, count, resid, upstream)


def exchange(rows, axes):
    return lax.all_to_all(rows, axes, split_axis=0, concat_axis=0, tiled=True)


def local(
    frames,
    cotangent,
    lengths,
    qkv_weight,
    out_weight,
    router,
    expert_in,
    expert_out,
    send_index,
    send_count,
):
    own_frames = frames[0]
    upstream = cotangent[0]
    index = send_index[0].T
    everywhere = ("seq", "exp")

    parts = project(own_frames, qkv_weight).reshape(HEADS, PART, FR)
    parts = exchange(parts, "seq").reshape(HEADS * PART, FR)
    packed = gather_rows(upstream, index, send_count)
    attended = attend(lengths, parts).reshape(HEADS, HD, FR)
    attended = exchange(attended, "seq").reshape(HALF, FR)
    resid, packed = residual(attended, own_frames, out_weight, index, send_count, packed)
    arrived = exchange(packed, everywhere)
    back, picked, active, before_grad, out_grad, grad_route = expert(
        arrived, expert_in[0], expert_out[0], router
    )
    arrived_back = exchange(back, everywhere)
    grad_first, grad_second = weight_grads(picked, before_grad, active, out_grad)
    output, grad_resid = combine(arrived_back, index, send_count, resid, upstream)
    return (output[None], grad_resid[None], grad_first[None], grad_second[None], grad_route)


def solution(mesh):
    in_specs = (
        P("exp", "seq", None),
        P("exp", "seq", None),
        P("exp"),
        P(),
        P(),
        P(("seq", "exp"), None),
        P(("seq", "exp"), None, None),
        P(("seq", "exp"), None, None),
        P(("seq", "exp"), None, None),
        P(("seq", "exp"), None),
    )
    out_specs = (
        P("exp", "seq", None),
        P("exp", "seq", None),
        P(("seq", "exp"), None, None),
        P(("seq", "exp"), None, None),
        P(("seq", "exp"), None),
    )
    return jax.shard_map(local, mesh=mesh, in_specs=in_specs, out_specs=out_specs, check_vma=False)
```

```python
import jax
import jax.numpy as jnp
from jax import lax
from jax.experimental import pallas as pl
from jax.experimental.pallas import tpu as pltpu
from jax.sharding import PartitionSpec as P

HEADS = 8
HD = 64
D = 1024
FF = 2048
FR = 128
DEVS = 128
SLOT = 3
KEYS = 1024
LIVE = 256
TILES = D // 128
ROWS = SLOT * TILES

epsilon = 1e-05
masked_score = -1e30
empty_mark = 2.0**100
empty_bound = 2.0**99

F32 = jnp.float32
BF16 = jnp.bfloat16
MB = 1024 * 1024


def params(mib):
    return pltpu.CompilerParams(vmem_limit_bytes=mib * MB)


def whole(shape):
    return pl.BlockSpec(shape, lambda *_: (0,) * len(shape))


def dot(a, b, dims=((1,), (0,))):
    return lax.dot_general(a, b, (dims, ((), ())), preferred_element_type=F32)


def normalize(values):
    center = jnp.mean(values, axis=-1, keepdims=True)
    shifted = values - center
    spread = jnp.mean(jnp.square(shifted), axis=-1, keepdims=True)
    inverse = lax.rsqrt(spread + epsilon)
    return shifted * inverse, inverse


def spread_matrix(index_ref, count_ref, slot):
    frame = lax.broadcasted_iota(jnp.int32, (FR, DEVS), 0)
    named = jnp.broadcast_to(index_ref[slot : slot + 1, :], (FR, DEVS)) == frame
    used = jnp.broadcast_to(count_ref[...], (FR, DEVS)) > slot
    return jnp.where(named & used, 1.0, 0.0)


def pack_rows(stage, rows, slot):
    for tile in range(TILES):
        at = pl.ds(slot * TILES + tile, DEVS, stride=ROWS)
        stage[at, :] = rows[:, tile * 128 : (tile + 1) * 128]


def stage_rows(stage, rows_ref, half):
    stage[...] = rows_ref[:, half].astype(F32).reshape(DEVS * ROWS, 128)


def unpack_rows(stage, slot):
    tiles = [stage[pl.ds(slot * TILES + tile, DEVS, stride=ROWS), :] for tile in range(TILES)]
    return jnp.concatenate(tiles, axis=1)


PART = HD * 3
HALF = HEADS * HD


def project_kernel(frames_ref, weight_ref, out_ref, normed):
    step = pl.program_id(0)

    @pl.when(step == 0)
    def _():
        normed[...] = normalize(frames_ref[...].astype(F32))[0].astype(BF16)

    block = dot(normed[...], weight_ref[...]).T.astype(BF16)
    for head in range(HEADS):
        start = pl.multiple_of(head * PART + step * HD, HD)
        out_ref[pl.ds(start, HD), :] = block[head * HD : (head + 1) * HD]


def project(frames, weight):
    return pl.pallas_call(
        project_kernel,
        grid=(3,),
        in_specs=[whole((FR, D)), pl.BlockSpec((D, HALF), lambda n: (0, n))],
        out_specs=whole((HEADS * PART, FR)),
        out_shape=jax.ShapeDtypeStruct((HEADS * PART, FR), BF16),
        scratch_shapes=[pltpu.VMEM((FR, D), BF16)],
        compiler_params=params(56),
        cost_estimate=pl.CostEstimate(
            flops=2 * FR * D * 3 * HALF, bytes_accessed=4 * MB, transcendentals=0
        ),
    )(frames, weight)


def staged(stage):
    return stage[...].reshape(DEVS, 1, ROWS, 128).astype(BF16)


def gather_kernel(table_ref, index_ref, count_ref, out_ref, stage):
    count_column = jnp.broadcast_to(count_ref[...].astype(F32), (DEVS, DEVS)).T
    for slot in range(SLOT):
        pick = spread_matrix(index_ref, count_ref, slot).T.astype(BF16)
        rows = dot(pick, table_ref[...])
        mark = jnp.where(count_column[:, 0:1] > slot, 0.0, empty_mark)
        pack_rows(stage, rows + mark, slot)
    out_ref[...] = staged(stage)


def gather_rows(table, index, count):
    return pl.pallas_call(
        gather_kernel,
        grid=(1,),
        in_specs=[whole((FR, D)), whole((SLOT, DEVS)), whole((1, DEVS))],
        out_specs=pl.BlockSpec((DEVS, 1, ROWS, 128), lambda n: (0, 1, 0, 0)),
        out_shape=jax.ShapeDtypeStruct((DEVS, 2, ROWS, 128), BF16),
        scratch_shapes=[pltpu.VMEM((DEVS * ROWS, 128), F32)],
        compiler_params=params(20),
        cost_estimate=pl.CostEstimate(
            flops=2 * DEVS * SLOT * FR * D, bytes_accessed=2 * MB, transcendentals=0
        ),
    )(table, index, count)


QUERIES = 256


def attend_kernel(length_ref, parts_ref, out_ref):
    parts = [parts_ref[s * PART : (s + 1) * PART, :] for s in range(HEADS)]
    q = jnp.concatenate([part[:HD] for part in parts], axis=1)
    k = jnp.concatenate([part[HD : 2 * HD] for part in parts], axis=1).astype(F32)
    k = (k * HD ** (-0.5)).T.astype(BF16)
    v = jnp.concatenate([part[2 * HD :] for part in parts], axis=1)
    live = lax.broadcasted_iota(jnp.int32, (KEYS, QUERIES), 0) < length_ref[0]
    for first in range(0, KEYS, QUERIES):
        scores = dot(k, q[:, first : first + QUERIES])
        scores = jnp.where(live, scores, masked_score)
        top = jnp.max(scores, axis=0, keepdims=True)
        weights = jnp.exp(scores - top)
        total = jnp.sum(weights, axis=0, keepdims=True)
        mixed = (dot(v, weights.astype(BF16)) / total).astype(BF16)
        for piece in range(QUERIES // FR):
            source = first // FR + piece
            out_ref[source * HD : (source + 1) * HD, :] = mixed[:, piece * FR : (piece + 1) * FR]


def attend(length, parts):
    return pl.pallas_call(
        attend_kernel,
        in_specs=[
            pl.BlockSpec(memory_space=pltpu.SMEM),
            pl.BlockSpec(memory_space=pltpu.VMEM),
        ],
        out_shape=jax.ShapeDtypeStruct((HALF, FR), BF16),
        compiler_params=params(24),
        cost_estimate=pl.CostEstimate(
            flops=4 * KEYS * KEYS * HD, bytes_accessed=MB // 2, transcendentals=KEYS * KEYS
        ),
    )(length, parts)


def residual_kernel(
    attended_ref, frames_ref, weight_ref, index_ref, count_ref, packed_ref,
    resid_ref, out_ref, stage,
):
    attended = attended_ref[...].astype(F32).T.astype(BF16)
    resid = (frames_ref[...].astype(F32) + dot(attended, weight_ref[...])).astype(BF16)
    resid_ref[...] = resid
    mid = normalize(resid.astype(F32))[0].astype(BF16)
    for slot in range(SLOT):
        pick = spread_matrix(index_ref, count_ref, slot).T.astype(BF16)
        pack_rows(stage, dot(pick, mid), slot)
    out_ref[...] = staged(stage)


def residual(attended, frames, weight, index, count, packed):
    return pl.pallas_call(
        residual_kernel,
        grid=(1,),
        in_specs=[
            whole((HALF, FR)),
            whole((FR, D)),
            whole((HALF, D)),
            whole((SLOT, DEVS)),
            whole((1, DEVS)),
            pl.BlockSpec(memory_space=pl.ANY),
        ],
        out_specs=[
            whole((FR, D)),
            pl.BlockSpec((DEVS, 1, ROWS, 128), lambda n: (0, 0, 0, 0)),
        ],
        out_shape=[
            jax.ShapeDtypeStruct((FR, D), BF16),
            jax.ShapeDtypeStruct((DEVS, 2, ROWS, 128), BF16),
        ],
        input_output_aliases={5: 1},
        scratch_shapes=[pltpu.VMEM((DEVS * ROWS, 128), F32)],
        compiler_params=params(24),
        cost_estimate=pl.CostEstimate(
            flops=2 * FR * HALF * D + 2 * DEVS * SLOT * FR * D,
            bytes_accessed=3 * MB, transcendentals=0,
        ),
    )(attended, frames, weight, index, count, packed)


FF_TILE = 1024
FF_STEPS = FF // FF_TILE
WG_TILE = 512
gelu_scale = (2.0 / jnp.pi) ** 0.5
gelu_cubic = 0.044715


def seats(first_column):
    total = SLOT * DEVS
    live = first_column < empty_bound
    ahead = lax.broadcasted_iota(jnp.int32, (total, total), 0) >= lax.broadcasted_iota(
        jnp.int32, (total, total), 1
    )
    ranks = dot(jnp.where(ahead, 1.0, 0.0).astype(BF16), jnp.where(live, 1.0, 0.0).astype(BF16))
    seat = jnp.where(live, ranks - 1.0, -1.0)[:, 0:1].astype(jnp.int32)
    return jnp.where(seat == lax.broadcasted_iota(jnp.int32, (total, LIVE), 1), 1.0, 0.0)


def expert_kernel(
    rows_ref, first_hbm, second_hbm, router_ref,
    back_ref, route_grad_ref, saved_ref,
    stage_x, stage_g, pulled_ref, first_ref, second_ref, first_sem, second_sem,
):
    picked_ref = saved_ref.at[:, :D]
    out_grad_ref = saved_ref.at[:, D : 2 * D]
    active_ref = saved_ref.at[:, 2 * D : 2 * D + FF]
    before_grad_ref = saved_ref.at[:, 2 * D + FF :]

    def tiles(step):
        return pl.ds(step * FF_TILE, FF_TILE)

    first_loads, second_loads = [], []
    for step in range(FF_STEPS):
        columns = tiles(step)
        first_loads.append(pltpu.make_async_copy(
            first_hbm.at[:, columns], first_ref.at[:, columns], first_sem.at[step]
        ))
        second_loads.append(pltpu.make_async_copy(
            second_hbm.at[columns, :], second_ref.at[columns, :], second_sem.at[step]
        ))
        second_loads[-1].start()
        first_loads[-1].start()

    stage_rows(stage_g, rows_ref, 1)
    grads = jnp.concatenate([unpack_rows(stage_g, slot) for slot in range(SLOT)], axis=0)
    place = seats(grads[:, 0:128])
    take = place.T.astype(BF16)
    place = place.astype(BF16)
    grads = dot(take, grads.astype(BF16)).astype(BF16)
    for step in range(FF_STEPS):
        second_loads[step].wait()
        pulled_ref[:, tiles(step)] = dot(grads, second_ref[tiles(step), :], ((1,), (1,)))
    stage_rows(stage_x, rows_ref, 0)
    rows = [unpack_rows(stage_x, slot).astype(BF16) for slot in range(SLOT)]
    picked_wide = dot(take, jnp.concatenate(rows, axis=0))
    picked = picked_wide.astype(BF16)
    picked_ref[...] = picked
    logits = jnp.sum(picked_wide * router_ref[...], axis=-1, keepdims=True)
    gate = 1.0 / (1.0 + jnp.exp(-logits))
    out_grad_ref[...] = (gate * grads.astype(F32)).astype(BF16)

    logit = jnp.zeros((LIVE, 1), F32)
    for step in range(FF_STEPS):
        columns = tiles(step)
        pulled = pulled_ref[:, columns]
        first_loads[step].wait()
        before = dot(picked, first_ref[:, columns])
        square = before * before
        bend = jnp.tanh(before * (gelu_scale + (gelu_scale * gelu_cubic) * square))
        half = 0.5 + 0.5 * bend
        active = (before * half).astype(BF16)
        slope = half + (before * (1.0 - bend * bend)) * (
            0.5 * gelu_scale + (1.5 * gelu_scale * gelu_cubic) * square
        )
        active_ref[:, columns] = active
        before_grad_ref[:, columns] = (gate * pulled * slope).astype(BF16)
        logit += jnp.sum(active.astype(F32) * pulled, axis=-1, keepdims=True)

    logit_grad = logit * gate * (1.0 - gate)
    route_grad_ref[...] = jnp.sum(logit_grad * picked_ref[...].astype(F32), axis=0, keepdims=True)
    result = dot(active_ref[...], second_ref[...])
    returned = dot(place, (gate * result).astype(BF16))
    for slot in range(SLOT):
        pack_rows(stage_x, returned[slot * DEVS : (slot + 1) * DEVS], slot)
    back_ref[:, 0:1] = staged(stage_x)
    row_grad = dot(before_grad_ref[...], first_ref[...], ((1,), (1,)))
    row_grad = row_grad + logit_grad * router_ref[...]
    row_grad = dot(place, row_grad.astype(BF16))
    for slot in range(SLOT):
        pack_rows(stage_g, row_grad[slot * DEVS : (slot + 1) * DEVS], slot)
    back_ref[:, 1:2] = staged(stage_g)


def expert(rows, first, second, router):
    vmem = pl.BlockSpec(memory_space=pltpu.VMEM)
    hbm = pl.BlockSpec(memory_space=pl.ANY)
    return pl.pallas_call(
        expert_kernel,
        in_specs=[vmem, hbm, hbm, vmem],
        out_specs=[vmem, vmem, vmem],
        out_shape=[
            jax.ShapeDtypeStruct((DEVS, 2, ROWS, 128), BF16),
            jax.ShapeDtypeStruct((1, D), F32),
            jax.ShapeDtypeStruct((LIVE, 2 * D + 2 * FF), BF16),
        ],
        scratch_shapes=[
            pltpu.VMEM((DEVS * ROWS, 128), F32),
            pltpu.VMEM((DEVS * ROWS, 128), F32),
            pltpu.VMEM((LIVE, FF), F32),
            pltpu.VMEM((D, FF), BF16),
            pltpu.VMEM((FF, D), BF16),
            pltpu.SemaphoreType.DMA((FF_STEPS,)),
            pltpu.SemaphoreType.DMA((FF_STEPS,)),
        ],
        compiler_params=params(44),
        cost_estimate=pl.CostEstimate(
            flops=8 * LIVE * D * FF, bytes_accessed=14 * MB, transcendentals=LIVE * FF
        ),
    )(rows, first, second, router)


def weight_grad_kernel(picked_ref, before_grad_ref, active_ref, out_grad_ref, first_ref, second_ref):
    first_ref[...] = dot(picked_ref[...], before_grad_ref[...], ((0,), (0,))).astype(BF16)
    second_ref[...] = dot(active_ref[...], out_grad_ref[...], ((0,), (0,))).astype(BF16)


def weight_grads(saved):
    tile = WG_TILE
    return pl.pallas_call(
        weight_grad_kernel,
        grid=(FF // tile,),
        in_specs=[
            pl.BlockSpec((LIVE, D), lambda n: (0, 0)),
            pl.BlockSpec((LIVE, tile), lambda n: (0, (2 * D + FF) // tile + n)),
            pl.BlockSpec((LIVE, tile), lambda n: (0, 2 * D // tile + n)),
            pl.BlockSpec((LIVE, D), lambda n: (0, 1)),
        ],
        out_specs=[
            pl.BlockSpec((D, tile), lambda n: (0, n)),
            pl.BlockSpec((tile, D), lambda n: (n, 0)),
        ],
        out_shape=[
            jax.ShapeDtypeStruct((D, FF), BF16),
            jax.ShapeDtypeStruct((FF, D), BF16),
        ],
        compiler_params=params(24),
        cost_estimate=pl.CostEstimate(
            flops=4 * LIVE * D * FF, bytes_accessed=11 * MB, transcendentals=0
        ),
    )(saved, saved, saved, saved)


def combine_kernel(
    rows_ref, index_ref, count_ref, resid_ref, upstream_ref, output_ref, grad_ref, stage, stage_g
):
    stage_rows(stage, rows_ref, 0)
    stage_rows(stage_g, rows_ref, 1)
    mixture = jnp.zeros((FR, D), F32)
    normed_grad = jnp.zeros((FR, D), F32)
    for slot in range(SLOT):
        spread = spread_matrix(index_ref, count_ref, slot).astype(BF16)
        mixture += dot(spread, unpack_rows(stage, slot).astype(BF16))
        normed_grad += dot(spread, unpack_rows(stage_g, slot).astype(BF16))
    resid = resid_ref[...].astype(F32)
    output_ref[...] = (resid + mixture).astype(BF16)
    unit, inverse = normalize(resid)
    first_mean = jnp.mean(normed_grad, axis=-1, keepdims=True)
    second_mean = jnp.mean(normed_grad * unit, axis=-1, keepdims=True)
    grad = inverse * (normed_grad - first_mean - unit * second_mean)
    grad_ref[...] = (upstream_ref[...].astype(F32) + grad).astype(BF16)


def combine(rows, index, count, resid, upstream):
    return pl.pallas_call(
        combine_kernel,
        out_shape=[jax.ShapeDtypeStruct((FR, D), BF16)] * 2,
        scratch_shapes=[pltpu.VMEM((DEVS * ROWS, 128), F32)] * 2,
        compiler_params=params(28),
        cost_estimate=pl.CostEstimate(
            flops=4 * DEVS * SLOT * FR * D, bytes_accessed=3 * MB, transcendentals=0
        ),
    )(rows, index, count, resid, upstream)


def exchange(rows, axes):
    return lax.all_to_all(rows, axes, split_axis=0, concat_axis=0, tiled=True)


def local(
    frames,
    cotangent,
    lengths,
    qkv_weight,
    out_weight,
    router,
    expert_in,
    expert_out,
    send_index,
    send_count,
):
    own_frames = frames[0]
    upstream = cotangent[0]
    index = send_index[0].T
    everywhere = ("seq", "exp")

    parts = project(own_frames, qkv_weight).reshape(HEADS, PART, FR)
    parts = exchange(parts, "seq").reshape(HEADS * PART, FR)
    packed = gather_rows(upstream, index, send_count)
    attended = attend(lengths, parts).reshape(HEADS, HD, FR)
    attended = exchange(attended, "seq").reshape(HALF, FR)
    resid, packed = residual(attended, own_frames, out_weight, index, send_count, packed)
    arrived = exchange(packed, everywhere)
    back, grad_route, saved = expert(
        arrived, expert_in[0], expert_out[0], router
    )
    arrived_back = exchange(back, everywhere)
    grad_first, grad_second = weight_grads(saved)
    output, grad_resid = combine(arrived_back, index, send_count, resid, upstream)
    return (output[None], grad_resid[None], grad_first[None], grad_second[None], grad_route)


def solution(mesh):
    in_specs = (
        P("exp", "seq", None),
        P("exp", "seq", None),
        P("exp"),
        P(),
        P(),
        P(("seq", "exp"), None),
        P(("seq", "exp"), None, None),
        P(("seq", "exp"), None, None),
        P(("seq", "exp"), None, None),
        P(("seq", "exp"), None),
    )
    out_specs = (
        P("exp", "seq", None),
        P("exp", "seq", None),
        P(("seq", "exp"), None, None),
        P(("seq", "exp"), None, None),
        P(("seq", "exp"), None),
    )
    return jax.shard_map(local, mesh=mesh, in_specs=in_specs, out_specs=out_specs, check_vma=False)
```

```python
import jax
import jax.numpy as jnp
from jax import lax
from jax.experimental import pallas as pl
from jax.experimental.pallas import tpu as pltpu
from jax.sharding import PartitionSpec as P

HEADS = 8
HD = 64
D = 1024
FF = 2048
FR = 128
DEVS = 128
SLOT = 3
UTTS = 16
KEYS = 1024
LIVE = 256
TILES = D // 128
ROWS = SLOT * TILES

epsilon = 1e-05
masked_score = -1e30
empty_mark = 2.0**100
empty_bound = 2.0**99

F32 = jnp.float32
BF16 = jnp.bfloat16
MB = 1024 * 1024


def params(mib):
    return pltpu.CompilerParams(vmem_limit_bytes=mib * MB)


def whole(shape):
    return pl.BlockSpec(shape, lambda *_: (0,) * len(shape))


def dot(a, b, dims=((1,), (0,))):
    return lax.dot_general(a, b, (dims, ((), ())), preferred_element_type=F32)


def normalize(values):
    center = jnp.mean(values, axis=-1, keepdims=True)
    shifted = values - center
    spread = jnp.mean(jnp.square(shifted), axis=-1, keepdims=True)
    inverse = lax.rsqrt(spread + epsilon)
    return shifted * inverse, inverse


def spread_matrix(index_ref, count_ref, slot):
    frame = lax.broadcasted_iota(jnp.int32, (FR, DEVS), 0)
    named = jnp.broadcast_to(index_ref[slot : slot + 1, :], (FR, DEVS)) == frame
    used = jnp.broadcast_to(count_ref[...], (FR, DEVS)) > slot
    return jnp.where(named & used, 1.0, 0.0)


def pack_rows(stage, rows, slot):
    for tile in range(TILES):
        at = pl.ds(slot * TILES + tile, DEVS, stride=ROWS)
        stage[at, :] = rows[:, tile * 128 : (tile + 1) * 128]


def stage_rows(stage, rows_ref, half):
    stage[...] = rows_ref[:, half].astype(F32).reshape(DEVS * ROWS, 128)


def unpack_rows(stage, slot):
    tiles = [stage[pl.ds(slot * TILES + tile, DEVS, stride=ROWS), :] for tile in range(TILES)]
    return jnp.concatenate(tiles, axis=1)


INFO = 16
PART = HD * 3 + INFO
HALF = HEADS * HD


def project_kernel(frames_ref, index_ref, count_ref, weight_ref, out_ref, normed):
    step = pl.program_id(0)

    @pl.when(step == 0)
    def _():
        normed[...] = normalize(frames_ref[...].astype(F32))[0].astype(BF16)
        info = jnp.concatenate(
            [
                index_ref[...].astype(F32),
                count_ref[...].astype(F32),
                jnp.zeros((INFO - SLOT - 1, DEVS), F32),
            ],
            axis=0,
        ).astype(BF16)
        for head in range(HEADS):
            out_ref[head, 3 * HD :, :] = info

    block = dot(normed[...], weight_ref[...]).T.astype(BF16)
    for head in range(HEADS):
        start = pl.multiple_of(step * HD, HD)
        out_ref[head, pl.ds(start, HD), :] = block[head * HD : (head + 1) * HD]


def project(frames, index, count, weight):
    return pl.pallas_call(
        project_kernel,
        grid=(3,),
        in_specs=[
            whole((FR, D)),
            whole((SLOT, DEVS)),
            whole((1, DEVS)),
            pl.BlockSpec((D, HALF), lambda n: (0, n)),
        ],
        out_specs=whole((HEADS, PART, FR)),
        out_shape=jax.ShapeDtypeStruct((HEADS, PART, FR), BF16),
        scratch_shapes=[pltpu.VMEM((FR, D), BF16)],
        compiler_params=params(56),
        cost_estimate=pl.CostEstimate(
            flops=2 * FR * D * 3 * HALF, bytes_accessed=4 * MB, transcendentals=0
        ),
    )(frames, index, count, weight)


SENT = 64
ATTENDED = 16
ATTENDED_ROWS = slice(SENT - ATTENDED, SENT)


def staged(stage):
    return stage[...].reshape(DEVS, ROWS, 128)


def gather_kernel(grads_ref, frames_ref, index_ref, count_ref, out_ref, stage_g, stage_f):
    count_column = jnp.broadcast_to(count_ref[...].astype(F32), (DEVS, DEVS)).T
    for slot in range(SLOT):
        pick = spread_matrix(index_ref, count_ref, slot).T.astype(BF16)
        mark = jnp.where(count_column[:, 0:1] > slot, 0.0, empty_mark)
        pack_rows(stage_g, dot(pick, grads_ref[...]) + mark, slot)
        pack_rows(stage_f, dot(pick, frames_ref[...]), slot)
    rows = jnp.concatenate([staged(stage_g), staged(stage_f)], axis=1)
    out_ref[...] = rows.astype(BF16)


def gather_rows(grads, frames, index, count):
    return pl.pallas_call(
        gather_kernel,
        grid=(1,),
        in_specs=[whole((FR, D)), whole((FR, D)), whole((SLOT, DEVS)), whole((1, DEVS))],
        out_specs=pl.BlockSpec((DEVS, 2 * ROWS, 128), lambda n: (0, 0, 0)),
        out_shape=jax.ShapeDtypeStruct((DEVS, SENT, 128), BF16),
        scratch_shapes=[pltpu.VMEM((DEVS * ROWS, 128), F32)] * 2,
        compiler_params=params(24),
        cost_estimate=pl.CostEstimate(
            flops=4 * DEVS * SLOT * FR * D, bytes_accessed=3 * MB, transcendentals=0
        ),
    )(grads, frames, index, count)


QUERIES = 256


def attend_kernel(scalar_ref, parts_ref, packed_ref, out_ref, sent_ref, stage):
    parts = [parts_ref[s] for s in range(HEADS)]
    q = jnp.concatenate([part[:HD] for part in parts], axis=1)
    k = jnp.concatenate([part[HD : 2 * HD] for part in parts], axis=1).astype(F32)
    k = (k * HD ** (-0.5)).T.astype(BF16)
    v = jnp.concatenate([part[2 * HD : 3 * HD] for part in parts], axis=1)
    infos = [part[3 * HD :].astype(F32) for part in parts]
    live = lax.broadcasted_iota(jnp.int32, (KEYS, QUERIES), 0) < scalar_ref[0]
    head = scalar_ref[1]
    frame = lax.broadcasted_iota(jnp.int32, (FR, DEVS), 0).astype(F32)
    upper = lax.broadcasted_iota(jnp.int32, (2 * HD, QUERIES), 0) < HD
    own = upper == (lax.broadcasted_iota(jnp.int32, (2 * HD, QUERIES), 1) < FR)
    stage[...] = jnp.zeros_like(stage)

    def spread(source, slot):
        info = infos[source]
        named = jnp.broadcast_to(info[slot : slot + 1], (FR, DEVS)) == frame
        used = jnp.broadcast_to(info[SLOT : SLOT + 1], (FR, DEVS)) > slot
        return jnp.where(named & used, 1.0, 0.0)

    for pair in range(KEYS // QUERIES):
        scores = dot(k, q[:, pair * QUERIES : (pair + 1) * QUERIES])
        scores = jnp.where(live, scores, masked_score)
        top = jnp.max(scores, axis=0, keepdims=True)
        weights = jnp.exp(scores - top)
        total = jnp.sum(weights, axis=0, keepdims=True)
        mixed = (dot(v, weights.astype(BF16)) / total).astype(BF16)
        for half in range(2):
            source = 2 * pair + half
            piece = lax.rem(source - head + HEADS, HEADS)
            out_ref[piece] = mixed[:, half * FR : (half + 1) * FR]
        mixed = mixed.astype(F32)
        twice = jnp.where(own, jnp.concatenate([mixed, mixed], axis=0), 0.0).astype(BF16)
        for slot in range(SLOT):
            spreads = [spread(2 * pair, slot), spread(2 * pair + 1, slot)]
            spreads = jnp.concatenate(spreads, axis=0).astype(BF16)
            at = pl.ds(slot * (KEYS // QUERIES) + pair, DEVS, stride=ATTENDED)
            stage[at, :] = dot(twice, spreads).T
    sent_ref[...] = stage[...].reshape(DEVS, ATTENDED, 128).astype(BF16)


def attend(scalars, parts, packed):
    return pl.pallas_call(
        attend_kernel,
        grid=(1,),
        in_specs=[
            pl.BlockSpec(memory_space=pltpu.SMEM),
            whole((HEADS, PART, FR)),
            pl.BlockSpec(memory_space=pl.ANY),
        ],
        out_specs=[
            whole((HEADS, HD, FR)),
            pl.BlockSpec((DEVS, ATTENDED, 128), lambda n: (0, SENT // ATTENDED - 1, 0)),
        ],
        out_shape=[
            jax.ShapeDtypeStruct((HEADS, HD, FR), BF16),
            jax.ShapeDtypeStruct((DEVS, SENT, 128), BF16),
        ],
        input_output_aliases={2: 1},
        scratch_shapes=[pltpu.VMEM((DEVS * ATTENDED, 128), F32)],
        compiler_params=params(28),
        cost_estimate=pl.CostEstimate(
            flops=4 * KEYS * KEYS * HD, bytes_accessed=MB, transcendentals=KEYS * KEYS
        ),
    )(scalars, parts, packed)


def residual_kernel(scalar_ref, *refs):
    pieces, (frames_ref, weight_ref, resid_ref, attended) = refs[:HEADS], refs[HEADS:]
    for step in range(HEADS):
        head = lax.rem(scalar_ref[1] - step + HEADS, HEADS)
        attended[pl.ds(pl.multiple_of(head * HD, HD), HD), :] = pieces[step][...]
    mixed = dot(attended[...].astype(F32).T.astype(BF16), weight_ref[...])
    resid_ref[...] = (frames_ref[...].astype(F32) + mixed).astype(BF16)


def residual(scalars, pieces, frames, weight):
    vmem = pl.BlockSpec(memory_space=pltpu.VMEM)
    return pl.pallas_call(
        residual_kernel,
        in_specs=[pl.BlockSpec(memory_space=pltpu.SMEM)] + [vmem] * (HEADS + 2),
        out_specs=vmem,
        out_shape=jax.ShapeDtypeStruct((FR, D), BF16),
        scratch_shapes=[pltpu.VMEM((HALF, FR), BF16)],
        compiler_params=params(16),
        cost_estimate=pl.CostEstimate(
            flops=2 * FR * HALF * D, bytes_accessed=2 * MB, transcendentals=0
        ),
    )(scalars, *pieces, frames, weight)


FF_TILE = 1024
FF_STEPS = FF // FF_TILE
WG_TILE = 512
gelu_scale = (2.0 / jnp.pi) ** 0.5
gelu_cubic = 0.044715


def seats(first_column):
    total = SLOT * DEVS
    live = first_column < empty_bound
    ahead = lax.broadcasted_iota(jnp.int32, (total, total), 0) >= lax.broadcasted_iota(
        jnp.int32, (total, total), 1
    )
    ranks = dot(jnp.where(ahead, 1.0, 0.0).astype(BF16), jnp.where(live, 1.0, 0.0).astype(BF16))
    seat = jnp.where(live, ranks - 1.0, -1.0)[:, 0:1].astype(jnp.int32)
    return jnp.where(seat == lax.broadcasted_iota(jnp.int32, (total, LIVE), 1), 1.0, 0.0)


def unpack_attended(stage):
    low = lax.broadcasted_iota(jnp.int32, (UTTS, 128), 1) < HD
    rows = []
    for slot in range(SLOT):
        for pair in range(HEADS // 2):
            at = pl.ds(slot * (HEADS // 2) + pair, DEVS, stride=ATTENDED)
            values = stage[at, :]
            heads = [values[head * UTTS : (head + 1) * UTTS] for head in range(HEADS)]
            for half in range(2):
                own = low if half == 0 else jnp.logical_not(low)
                kept = [jnp.where(own, part, 0.0) for part in heads]
                rows.append(jnp.concatenate(kept, axis=1))
    return jnp.concatenate(rows, axis=0).astype(BF16)


def expert_kernel(
    rows_ref, first_hbm, second_hbm, mix_hbm, router_ref,
    back_ref, route_grad_ref, saved_ref,
    stage_x, stage_g, stage_a, pulled_ref, first_ref, second_ref, mix_ref,
    first_sem, second_sem, mix_sem,
):
    picked_ref = saved_ref.at[:, :D]
    out_grad_ref = saved_ref.at[:, D : 2 * D]
    active_ref = saved_ref.at[:, 2 * D : 2 * D + FF]
    before_grad_ref = saved_ref.at[:, 2 * D + FF :]

    def tiles(step):
        return pl.ds(step * FF_TILE, FF_TILE)

    mix_load = pltpu.make_async_copy(mix_hbm, mix_ref, mix_sem)
    mix_load.start()
    first_loads, second_loads = [], []
    for step in range(FF_STEPS):
        columns = tiles(step)
        first_loads.append(pltpu.make_async_copy(
            first_hbm.at[:, columns], first_ref.at[:, columns], first_sem.at[step]
        ))
        second_loads.append(pltpu.make_async_copy(
            second_hbm.at[columns, :], second_ref.at[columns, :], second_sem.at[step]
        ))
        second_loads[-1].start()
        first_loads[-1].start()

    sent = rows_ref[...].astype(F32)
    stage_g[...] = sent[:, :ROWS].reshape(DEVS * ROWS, 128)
    stage_x[...] = sent[:, ROWS : 2 * ROWS].reshape(DEVS * ROWS, 128)
    stage_a[...] = sent[:, ATTENDED_ROWS].reshape(DEVS * ATTENDED, 128)
    grads = jnp.concatenate([unpack_rows(stage_g, slot) for slot in range(SLOT)], axis=0)
    place = seats(grads[:, 0:128])
    take = place.T.astype(BF16)
    place = place.astype(BF16)
    grads = dot(take, grads.astype(BF16)).astype(BF16)
    for step in range(FF_STEPS):
        second_loads[step].wait()
        pulled_ref[:, tiles(step)] = dot(grads, second_ref[tiles(step), :], ((1,), (1,)))
    rows = [unpack_rows(stage_x, slot).astype(BF16) for slot in range(SLOT)]
    taken = dot(take, jnp.concatenate(rows, axis=0))
    attended = dot(take, unpack_attended(stage_a))
    attended = [attended[:, head * 128 : (head + 1) * 128] for head in range(HEADS)]
    attended = [values + pltpu.roll(values, HD, 1) for values in attended]
    low = lax.broadcasted_iota(jnp.int32, (LIVE, 128), 1) < HD
    attended = [
        jnp.where(low, attended[head], attended[head + 1]) for head in range(0, HEADS, 2)
    ]
    attended = jnp.concatenate(attended, axis=1).astype(BF16)
    mix_load.wait()
    resid = (taken + dot(attended, mix_ref[...])).astype(BF16)
    picked = normalize(resid.astype(F32))[0].astype(BF16)
    picked_wide = picked.astype(F32)
    picked_ref[...] = picked
    logits = jnp.sum(picked_wide * router_ref[...], axis=-1, keepdims=True)
    gate = 1.0 / (1.0 + jnp.exp(-logits))
    out_grad_ref[...] = (gate * grads.astype(F32)).astype(BF16)

    logit = jnp.zeros((LIVE, 1), F32)
    for step in range(FF_STEPS):
        columns = tiles(step)
        pulled = pulled_ref[:, columns]
        first_loads[step].wait()
        before = dot(picked, first_ref[:, columns])
        square = before * before
        bend = jnp.tanh(before * (gelu_scale + (gelu_scale * gelu_cubic) * square))
        half = 0.5 + 0.5 * bend
        active = (before * half).astype(BF16)
        slope = half + (before * (1.0 - bend * bend)) * (
            0.5 * gelu_scale + (1.5 * gelu_scale * gelu_cubic) * square
        )
        active_ref[:, columns] = active
        before_grad_ref[:, columns] = (gate * pulled * slope).astype(BF16)
        logit += jnp.sum(active.astype(F32) * pulled, axis=-1, keepdims=True)

    logit_grad = logit * gate * (1.0 - gate)
    route_grad_ref[...] = jnp.sum(logit_grad * picked_ref[...].astype(F32), axis=0, keepdims=True)
    result = dot(active_ref[...], second_ref[...])
    returned = dot(place, (gate * result).astype(BF16))
    for slot in range(SLOT):
        pack_rows(stage_x, returned[slot * DEVS : (slot + 1) * DEVS], slot)
    back_ref[:, 0] = staged(stage_x).astype(BF16)
    row_grad = dot(before_grad_ref[...], first_ref[...], ((1,), (1,)))
    row_grad = row_grad + logit_grad * router_ref[...]
    row_grad = dot(place, row_grad.astype(BF16))
    for slot in range(SLOT):
        pack_rows(stage_g, row_grad[slot * DEVS : (slot + 1) * DEVS], slot)
    back_ref[:, 1] = staged(stage_g).astype(BF16)


def expert(rows, first, second, mix, router):
    vmem = pl.BlockSpec(memory_space=pltpu.VMEM)
    hbm = pl.BlockSpec(memory_space=pl.ANY)
    return pl.pallas_call(
        expert_kernel,
        in_specs=[vmem, hbm, hbm, hbm, vmem],
        out_specs=[vmem, vmem, vmem],
        out_shape=[
            jax.ShapeDtypeStruct((DEVS, 2, ROWS, 128), BF16),
            jax.ShapeDtypeStruct((1, D), F32),
            jax.ShapeDtypeStruct((LIVE, 2 * D + 2 * FF), BF16),
        ],
        scratch_shapes=[
            pltpu.VMEM((DEVS * ROWS, 128), F32),
            pltpu.VMEM((DEVS * ROWS, 128), F32),
            pltpu.VMEM((DEVS * ATTENDED, 128), F32),
            pltpu.VMEM((LIVE, FF), F32),
            pltpu.VMEM((D, FF), BF16),
            pltpu.VMEM((FF, D), BF16),
            pltpu.VMEM((HALF, D), BF16),
            pltpu.SemaphoreType.DMA((FF_STEPS,)),
            pltpu.SemaphoreType.DMA((FF_STEPS,)),
            pltpu.SemaphoreType.DMA,
        ],
        compiler_params=params(44),
        cost_estimate=pl.CostEstimate(
            flops=8 * LIVE * D * FF, bytes_accessed=14 * MB, transcendentals=LIVE * FF
        ),
    )(rows, first, second, mix, router)


def weight_grad_kernel(picked_ref, before_grad_ref, active_ref, out_grad_ref, first_ref, second_ref):
    first_ref[...] = dot(picked_ref[...], before_grad_ref[...], ((0,), (0,))).astype(BF16)
    second_ref[...] = dot(active_ref[...], out_grad_ref[...], ((0,), (0,))).astype(BF16)


def weight_grads(saved):
    tile = WG_TILE
    return pl.pallas_call(
        weight_grad_kernel,
        grid=(FF // tile,),
        in_specs=[
            pl.BlockSpec((LIVE, D), lambda n: (0, 0)),
            pl.BlockSpec((LIVE, tile), lambda n: (0, (2 * D + FF) // tile + n)),
            pl.BlockSpec((LIVE, tile), lambda n: (0, 2 * D // tile + n)),
            pl.BlockSpec((LIVE, D), lambda n: (0, 1)),
        ],
        out_specs=[
            pl.BlockSpec((D, tile), lambda n: (0, n)),
            pl.BlockSpec((tile, D), lambda n: (n, 0)),
        ],
        out_shape=[
            jax.ShapeDtypeStruct((D, FF), BF16),
            jax.ShapeDtypeStruct((FF, D), BF16),
        ],
        compiler_params=params(24),
        cost_estimate=pl.CostEstimate(
            flops=4 * LIVE * D * FF, bytes_accessed=11 * MB, transcendentals=0
        ),
    )(saved, saved, saved, saved)


def combine_kernel(
    rows_ref, index_ref, count_ref, resid_ref, upstream_ref, output_ref, grad_ref, stage, stage_g
):
    stage_rows(stage, rows_ref, 0)
    stage_rows(stage_g, rows_ref, 1)
    mixture = jnp.zeros((FR, D), F32)
    normed_grad = jnp.zeros((FR, D), F32)
    for slot in range(SLOT):
        spread = spread_matrix(index_ref, count_ref, slot).astype(BF16)
        mixture += dot(spread, unpack_rows(stage, slot).astype(BF16))
        normed_grad += dot(spread, unpack_rows(stage_g, slot).astype(BF16))
    resid = resid_ref[...].astype(F32)
    output_ref[...] = (resid + mixture).astype(BF16)
    unit, inverse = normalize(resid)
    first_mean = jnp.mean(normed_grad, axis=-1, keepdims=True)
    second_mean = jnp.mean(normed_grad * unit, axis=-1, keepdims=True)
    grad = inverse * (normed_grad - first_mean - unit * second_mean)
    grad_ref[...] = (upstream_ref[...].astype(F32) + grad).astype(BF16)


def combine(rows, index, count, resid, upstream):
    return pl.pallas_call(
        combine_kernel,
        out_shape=[jax.ShapeDtypeStruct((FR, D), BF16)] * 2,
        scratch_shapes=[pltpu.VMEM((DEVS * ROWS, 128), F32)] * 2,
        compiler_params=params(56),
        cost_estimate=pl.CostEstimate(
            flops=4 * DEVS * SLOT * FR * D, bytes_accessed=3 * MB, transcendentals=0
        ),
    )(rows, index, count, resid, upstream)


def exchange(rows, axes):
    return lax.all_to_all(rows, axes, split_axis=0, concat_axis=0, tiled=True)


def local(
    frames,
    cotangent,
    lengths,
    qkv_weight,
    out_weight,
    router,
    expert_in,
    expert_out,
    send_index,
    send_count,
):
    own_frames = frames[0]
    upstream = cotangent[0]
    index = send_index[0].T
    everywhere = ("seq", "exp")

    own = lax.axis_index("seq").astype(jnp.int32)
    scalars = jnp.concatenate([lengths, own[None]])

    parts = exchange(project(own_frames, index, send_count, qkv_weight), "seq")
    packed = gather_rows(upstream, own_frames, index, send_count)
    attended, packed = attend(scalars, parts, packed)
    arrived = exchange(packed, everywhere)
    pieces = [attended[0]]
    for step in range(1, HEADS):
        ring = [(source, (source + step) % HEADS) for source in range(HEADS)]
        pieces.append(lax.ppermute(attended[step], "seq", ring))
    resid = residual(scalars, pieces, own_frames, out_weight)
    back, grad_route, saved = expert(arrived, expert_in[0], expert_out[0], out_weight, router)
    arrived_back = exchange(back, everywhere)
    grad_first, grad_second = weight_grads(saved)
    output, grad_resid = combine(arrived_back, index, send_count, resid, upstream)
    return (output[None], grad_resid[None], grad_first[None], grad_second[None], grad_route)


def solution(mesh):
    in_specs = (
        P("exp", "seq", None),
        P("exp", "seq", None),
        P("exp"),
        P(),
        P(),
        P(("seq", "exp"), None),
        P(("seq", "exp"), None, None),
        P(("seq", "exp"), None, None),
        P(("seq", "exp"), None, None),
        P(("seq", "exp"), None),
    )
    out_specs = (
        P("exp", "seq", None),
        P("exp", "seq", None),
        P(("seq", "exp"), None, None),
        P(("seq", "exp"), None, None),
        P(("seq", "exp"), None),
    )
    return jax.shard_map(local, mesh=mesh, in_specs=in_specs, out_specs=out_specs, check_vma=False)
```

```python
import jax
import jax.numpy as jnp
from jax import lax
from jax.experimental import pallas as pl
from jax.experimental.pallas import tpu as pltpu
from jax.sharding import PartitionSpec as P

HEADS = 8
HD = 64
D = 1024
FF = 2048
FR = 128
DEVS = 128
SLOT = 3
UTTS = 16
KEYS = 1024
LIVE = 256
TILES = D // 128
ROWS = SLOT * TILES

epsilon = 1e-05
masked_score = -1e30
empty_mark = 2.0**100
empty_bound = 2.0**99

F32 = jnp.float32
BF16 = jnp.bfloat16
MB = 1024 * 1024


def params(mib):
    return pltpu.CompilerParams(vmem_limit_bytes=mib * MB)


def whole(shape):
    return pl.BlockSpec(shape, lambda *_: (0,) * len(shape))


def dot(a, b, dims=((1,), (0,))):
    return lax.dot_general(a, b, (dims, ((), ())), preferred_element_type=F32)


def normalize(values):
    center = jnp.mean(values, axis=-1, keepdims=True)
    shifted = values - center
    spread = jnp.mean(jnp.square(shifted), axis=-1, keepdims=True)
    inverse = lax.rsqrt(spread + epsilon)
    return shifted * inverse, inverse


def spread_matrix(index_ref, count_ref, slot):
    frame = lax.broadcasted_iota(jnp.int32, (FR, DEVS), 0)
    named = jnp.broadcast_to(index_ref[slot], (FR, DEVS)) == frame
    used = jnp.broadcast_to(count_ref[...], (FR, DEVS)) > slot
    return jnp.where(named & used, 1.0, 0.0)


def pack_rows(stage, rows, slot):
    for tile in range(TILES):
        at = pl.ds(slot * TILES + tile, DEVS, stride=ROWS)
        stage[at, :] = rows[:, tile * 128 : (tile + 1) * 128]


def stage_rows(stage, rows_ref, half):
    stage[...] = rows_ref[:, half].astype(F32).reshape(DEVS * ROWS, 128)


def unpack_rows(stage, slot):
    tiles = [stage[pl.ds(slot * TILES + tile, DEVS, stride=ROWS), :] for tile in range(TILES)]
    return jnp.concatenate(tiles, axis=1)


INFO = 16
PART = HD * 3 + INFO
HALF = HEADS * HD


def project_kernel(frames_ref, index_ref, count_ref, weight_ref, out_ref, normed):
    step = pl.program_id(0)

    @pl.when(step == 0)
    def _():
        normed[...] = normalize(frames_ref[...].astype(F32))[0].astype(BF16)
        info = jnp.concatenate(
            [
                *[index_ref[slot].astype(F32) for slot in range(SLOT)],
                count_ref[...].astype(F32),
                jnp.zeros((INFO - SLOT - 1, DEVS), F32),
            ],
            axis=0,
        ).astype(BF16)
        for head in range(HEADS):
            out_ref[head, 3 * HD :, :] = info

    block = dot(normed[...], weight_ref[...]).T.astype(BF16)
    for head in range(HEADS):
        start = pl.multiple_of(step * HD, HD)
        out_ref[head, pl.ds(start, HD), :] = block[head * HD : (head + 1) * HD]


def project(frames, index, count, weight):
    return pl.pallas_call(
        project_kernel,
        grid=(3,),
        in_specs=[
            whole((FR, D)),
            whole((SLOT, 1, DEVS)),
            whole((1, DEVS)),
            pl.BlockSpec((D, HALF), lambda n: (0, n)),
        ],
        out_specs=whole((HEADS, PART, FR)),
        out_shape=jax.ShapeDtypeStruct((HEADS, PART, FR), BF16),
        scratch_shapes=[pltpu.VMEM((FR, D), BF16)],
        compiler_params=params(56),
        cost_estimate=pl.CostEstimate(
            flops=2 * FR * D * 3 * HALF, bytes_accessed=4 * MB, transcendentals=0
        ),
    )(frames, index, count, weight)


SENT = 64
ATTENDED = 16
ATTENDED_ROWS = slice(SENT - ATTENDED, SENT)


def staged(stage):
    return stage[...].reshape(DEVS, ROWS, 128)


def gather_kernel(grads_ref, frames_ref, index_ref, count_ref, out_ref, stage_g, stage_f):
    count_column = jnp.broadcast_to(count_ref[...].astype(F32), (DEVS, DEVS)).T
    for slot in range(SLOT):
        pick = spread_matrix(index_ref, count_ref, slot).T.astype(BF16)
        mark = jnp.where(count_column[:, 0:1] > slot, 0.0, empty_mark)
        pack_rows(stage_g, dot(pick, grads_ref[...]) + mark, slot)
        pack_rows(stage_f, dot(pick, frames_ref[...]), slot)
    rows = jnp.concatenate([staged(stage_g), staged(stage_f)], axis=1)
    out_ref[...] = rows.astype(BF16)


def gather_rows(grads, frames, index, count):
    return pl.pallas_call(
        gather_kernel,
        grid=(1,),
        in_specs=[whole((FR, D)), whole((FR, D)), whole((SLOT, 1, DEVS)), whole((1, DEVS))],
        out_specs=pl.BlockSpec((DEVS, 2 * ROWS, 128), lambda n: (0, 0, 0)),
        out_shape=jax.ShapeDtypeStruct((DEVS, SENT, 128), BF16),
        scratch_shapes=[pltpu.VMEM((DEVS * ROWS, 128), F32)] * 2,
        compiler_params=params(24),
        cost_estimate=pl.CostEstimate(
            flops=4 * DEVS * SLOT * FR * D, bytes_accessed=3 * MB, transcendentals=0
        ),
    )(grads, frames, index, count)


QUERIES = 256


def attend_kernel(scalar_ref, parts_ref, packed_ref, out_ref, sent_ref, stage):
    parts = [parts_ref[s] for s in range(HEADS)]
    q = jnp.concatenate([part[:HD] for part in parts], axis=1)
    k = jnp.concatenate([part[HD : 2 * HD] for part in parts], axis=1).astype(F32)
    k = (k * HD ** (-0.5)).T.astype(BF16)
    v = jnp.concatenate([part[2 * HD : 3 * HD] for part in parts], axis=1)
    infos = [part[3 * HD :].astype(F32) for part in parts]
    live = lax.broadcasted_iota(jnp.int32, (KEYS, QUERIES), 0) < scalar_ref[0]
    head = scalar_ref[1]
    frame = lax.broadcasted_iota(jnp.int32, (FR, DEVS), 0).astype(F32)
    upper = lax.broadcasted_iota(jnp.int32, (2 * HD, QUERIES), 0) < HD
    own = upper == (lax.broadcasted_iota(jnp.int32, (2 * HD, QUERIES), 1) < FR)
    stage[...] = jnp.zeros_like(stage)

    def spread(source, slot):
        info = infos[source]
        named = jnp.broadcast_to(info[slot : slot + 1], (FR, DEVS)) == frame
        used = jnp.broadcast_to(info[SLOT : SLOT + 1], (FR, DEVS)) > slot
        return jnp.where(named & used, 1.0, 0.0)

    for pair in range(KEYS // QUERIES):
        scores = dot(k, q[:, pair * QUERIES : (pair + 1) * QUERIES])
        scores = jnp.where(live, scores, masked_score)
        top = jnp.max(scores, axis=0, keepdims=True)
        weights = jnp.exp(scores - top)
        total = jnp.sum(weights, axis=0, keepdims=True)
        mixed = (dot(v, weights.astype(BF16)) / total).astype(BF16)
        for half in range(2):
            source = 2 * pair + half
            piece = lax.rem(source - head + HEADS, HEADS)
            out_ref[piece] = mixed[:, half * FR : (half + 1) * FR]
        mixed = mixed.astype(F32)
        twice = jnp.where(own, jnp.concatenate([mixed, mixed], axis=0), 0.0).astype(BF16)
        for slot in range(SLOT):
            spreads = [spread(2 * pair, slot), spread(2 * pair + 1, slot)]
            spreads = jnp.concatenate(spreads, axis=0).astype(BF16)
            at = pl.ds(slot * (KEYS // QUERIES) + pair, DEVS, stride=ATTENDED)
            stage[at, :] = dot(twice, spreads).T
    sent_ref[...] = stage[...].reshape(DEVS, ATTENDED, 128).astype(BF16)


def attend(scalars, parts, packed):
    return pl.pallas_call(
        attend_kernel,
        grid=(1,),
        in_specs=[
            pl.BlockSpec(memory_space=pltpu.SMEM),
            whole((HEADS, PART, FR)),
            pl.BlockSpec(memory_space=pl.ANY),
        ],
        out_specs=[
            whole((HEADS, HD, FR)),
            pl.BlockSpec((DEVS, ATTENDED, 128), lambda n: (0, SENT // ATTENDED - 1, 0)),
        ],
        out_shape=[
            jax.ShapeDtypeStruct((HEADS, HD, FR), BF16),
            jax.ShapeDtypeStruct((DEVS, SENT, 128), BF16),
        ],
        input_output_aliases={2: 1},
        scratch_shapes=[pltpu.VMEM((DEVS * ATTENDED, 128), F32)],
        compiler_params=params(28),
        cost_estimate=pl.CostEstimate(
            flops=4 * KEYS * KEYS * HD, bytes_accessed=MB, transcendentals=KEYS * KEYS
        ),
    )(scalars, parts, packed)


def residual_kernel(scalar_ref, *refs):
    pieces, (frames_ref, weight_ref, resid_ref, attended) = refs[:HEADS], refs[HEADS:]
    for step in range(HEADS):
        head = lax.rem(scalar_ref[1] - step + HEADS, HEADS)
        attended[pl.ds(pl.multiple_of(head * HD, HD), HD), :] = pieces[step][...]
    mixed = dot(attended[...].astype(F32).T.astype(BF16), weight_ref[...])
    resid_ref[...] = (frames_ref[...].astype(F32) + mixed).astype(BF16)


def residual(scalars, pieces, frames, weight):
    vmem = pl.BlockSpec(memory_space=pltpu.VMEM)
    return pl.pallas_call(
        residual_kernel,
        in_specs=[pl.BlockSpec(memory_space=pltpu.SMEM)] + [vmem] * (HEADS + 2),
        out_specs=vmem,
        out_shape=jax.ShapeDtypeStruct((FR, D), BF16),
        scratch_shapes=[pltpu.VMEM((HALF, FR), BF16)],
        compiler_params=params(16),
        cost_estimate=pl.CostEstimate(
            flops=2 * FR * HALF * D, bytes_accessed=2 * MB, transcendentals=0
        ),
    )(scalars, *pieces, frames, weight)


FF_TILE = 1024
FF_STEPS = FF // FF_TILE
WG_TILE = 512
gelu_scale = (2.0 / jnp.pi) ** 0.5
gelu_cubic = 0.044715


def seats(first_column):
    total = SLOT * DEVS
    live = first_column < empty_bound
    ahead = lax.broadcasted_iota(jnp.int32, (total, total), 0) >= lax.broadcasted_iota(
        jnp.int32, (total, total), 1
    )
    ranks = dot(jnp.where(ahead, 1.0, 0.0).astype(BF16), jnp.where(live, 1.0, 0.0).astype(BF16))
    seat = jnp.where(live, ranks - 1.0, -1.0)[:, 0:1].astype(jnp.int32)
    return jnp.where(seat == lax.broadcasted_iota(jnp.int32, (total, LIVE), 1), 1.0, 0.0)


def unpack_attended(stage):
    low = lax.broadcasted_iota(jnp.int32, (UTTS, 128), 1) < HD
    rows = []
    for slot in range(SLOT):
        for pair in range(HEADS // 2):
            at = pl.ds(slot * (HEADS // 2) + pair, DEVS, stride=ATTENDED)
            values = stage[at, :]
            heads = [values[head * UTTS : (head + 1) * UTTS] for head in range(HEADS)]
            for half in range(2):
                own = low if half == 0 else jnp.logical_not(low)
                kept = [jnp.where(own, part, 0.0) for part in heads]
                rows.append(jnp.concatenate(kept, axis=1))
    return jnp.concatenate(rows, axis=0).astype(BF16)


def expert_kernel(
    rows_ref, first_hbm, second_hbm, mix_hbm, router_ref, after_hbm,
    back_hbm, route_grad_ref, saved_hbm,
    stage_x, stage_g, stage_a, pulled_ref, first_ref, second_ref, mix_ref, saved_ref, back_ref,
    first_sem, second_sem, mix_sem, rows_sem, active_sem, before_grad_sem, back_sem,
):
    stores = []

    def save(start, size, sem):
        columns = pl.ds(start, size)
        stores.append(pltpu.make_async_copy(
            saved_ref.at[:, columns], saved_hbm.at[:, columns], sem
        ))
        stores[-1].start()

    def leave(stage, half):
        back_ref[half] = staged(stage).astype(BF16)
        stores.append(pltpu.make_async_copy(
            back_ref.at[half], back_hbm.at[:, half], back_sem.at[half]
        ))
        stores[-1].start()

    picked_ref = saved_ref.at[:, :D]
    out_grad_ref = saved_ref.at[:, D : 2 * D]
    active_ref = saved_ref.at[:, 2 * D : 2 * D + FF]
    before_grad_ref = saved_ref.at[:, 2 * D + FF :]

    def tiles(step):
        return pl.ds(step * FF_TILE, FF_TILE)

    mix_load = pltpu.make_async_copy(mix_hbm, mix_ref, mix_sem)
    mix_load.start()
    first_loads, second_loads = [], []
    for step in range(FF_STEPS):
        columns = tiles(step)
        first_loads.append(pltpu.make_async_copy(
            first_hbm.at[:, columns], first_ref.at[:, columns], first_sem.at[step]
        ))
        second_loads.append(pltpu.make_async_copy(
            second_hbm.at[columns, :], second_ref.at[columns, :], second_sem.at[step]
        ))
        second_loads[-1].start()
        first_loads[-1].start()

    sent = rows_ref[...].astype(F32)
    stage_g[...] = sent[:, :ROWS].reshape(DEVS * ROWS, 128)
    stage_x[...] = sent[:, ROWS : 2 * ROWS].reshape(DEVS * ROWS, 128)
    stage_a[...] = sent[:, ATTENDED_ROWS].reshape(DEVS * ATTENDED, 128)
    grads = jnp.concatenate([unpack_rows(stage_g, slot) for slot in range(SLOT)], axis=0)
    place = seats(grads[:, 0:128])
    take = place.T.astype(BF16)
    place = place.astype(BF16)
    grads = dot(take, grads.astype(BF16)).astype(BF16)
    for step in range(FF_STEPS):
        second_loads[step].wait()
        pulled_ref[:, tiles(step)] = dot(grads, second_ref[tiles(step), :], ((1,), (1,)))
    rows = [unpack_rows(stage_x, slot).astype(BF16) for slot in range(SLOT)]
    taken = dot(take, jnp.concatenate(rows, axis=0))
    attended = dot(take, unpack_attended(stage_a))
    attended = [attended[:, head * 128 : (head + 1) * 128] for head in range(HEADS)]
    attended = [values + pltpu.roll(values, HD, 1) for values in attended]
    low = lax.broadcasted_iota(jnp.int32, (LIVE, 128), 1) < HD
    attended = [
        jnp.where(low, attended[head], attended[head + 1]) for head in range(0, HEADS, 2)
    ]
    attended = jnp.concatenate(attended, axis=1).astype(BF16)
    mix_load.wait()
    resid = (taken + dot(attended, mix_ref[...])).astype(BF16)
    picked = normalize(resid.astype(F32))[0].astype(BF16)
    picked_wide = picked.astype(F32)
    picked_ref[...] = picked
    logits = jnp.sum(picked_wide * router_ref[...], axis=-1, keepdims=True)
    gate = 1.0 / (1.0 + jnp.exp(-logits))
    out_grad_ref[...] = (gate * grads.astype(F32)).astype(BF16)
    save(0, 2 * D, rows_sem)

    logit = jnp.zeros((LIVE, 1), F32)
    for step in range(FF_STEPS):
        columns = tiles(step)
        pulled = pulled_ref[:, columns]
        first_loads[step].wait()
        before = dot(picked, first_ref[:, columns])
        square = before * before
        bend = jnp.tanh(before * (gelu_scale + (gelu_scale * gelu_cubic) * square))
        half = 0.5 + 0.5 * bend
        active = (before * half).astype(BF16)
        slope = half + (before * (1.0 - bend * bend)) * (
            0.5 * gelu_scale + (1.5 * gelu_scale * gelu_cubic) * square
        )
        active_ref[:, columns] = active
        before_grad_ref[:, columns] = (gate * pulled * slope).astype(BF16)
        save(2 * D + step * FF_TILE, FF_TILE, active_sem.at[step])
        save(2 * D + FF + step * FF_TILE, FF_TILE, before_grad_sem.at[step])
        logit += jnp.sum(active.astype(F32) * pulled, axis=-1, keepdims=True)

    logit_grad = logit * gate * (1.0 - gate)
    route_grad_ref[...] = jnp.sum(logit_grad * picked_ref[...].astype(F32), axis=0, keepdims=True)
    result = dot(active_ref[...], second_ref[...])
    returned = dot(place, (gate * result).astype(BF16))
    for slot in range(SLOT):
        pack_rows(stage_x, returned[slot * DEVS : (slot + 1) * DEVS], slot)
    leave(stage_x, 0)
    row_grad = dot(before_grad_ref[...], first_ref[...], ((1,), (1,)))
    row_grad = row_grad + logit_grad * router_ref[...]
    row_grad = dot(place, row_grad.astype(BF16))
    for slot in range(SLOT):
        pack_rows(stage_g, row_grad[slot * DEVS : (slot + 1) * DEVS], slot)
    leave(stage_g, 1)
    for copy in stores:
        copy.wait()


def expert(rows, first, second, mix, router, after):
    vmem = pl.BlockSpec(memory_space=pltpu.VMEM)
    hbm = pl.BlockSpec(memory_space=pl.ANY)
    return pl.pallas_call(
        expert_kernel,
        in_specs=[vmem, hbm, hbm, hbm, vmem, hbm],
        out_specs=[hbm, vmem, hbm],
        out_shape=[
            jax.ShapeDtypeStruct((DEVS, 2, ROWS, 128), BF16),
            jax.ShapeDtypeStruct((1, D), F32),
            jax.ShapeDtypeStruct((LIVE, 2 * D + 2 * FF), BF16),
        ],
        scratch_shapes=[
            pltpu.VMEM((DEVS * ROWS, 128), F32),
            pltpu.VMEM((DEVS * ROWS, 128), F32),
            pltpu.VMEM((DEVS * ATTENDED, 128), F32),
            pltpu.VMEM((LIVE, FF), F32),
            pltpu.VMEM((D, FF), BF16),
            pltpu.VMEM((FF, D), BF16),
            pltpu.VMEM((HALF, D), BF16),
            pltpu.VMEM((LIVE, 2 * D + 2 * FF), BF16),
            pltpu.VMEM((2, DEVS, ROWS, 128), BF16),
            pltpu.SemaphoreType.DMA((FF_STEPS,)),
            pltpu.SemaphoreType.DMA((FF_STEPS,)),
            pltpu.SemaphoreType.DMA,
            pltpu.SemaphoreType.DMA,
            pltpu.SemaphoreType.DMA((FF_STEPS,)),
            pltpu.SemaphoreType.DMA((FF_STEPS,)),
            pltpu.SemaphoreType.DMA((2,)),
        ],
        compiler_params=params(56),
        cost_estimate=pl.CostEstimate(
            flops=8 * LIVE * D * FF, bytes_accessed=14 * MB, transcendentals=LIVE * FF
        ),
    )(rows, first, second, mix, router, after)


def weight_grad_kernel(picked_ref, before_grad_ref, active_ref, out_grad_ref, first_ref, second_ref):
    first_ref[...] = dot(picked_ref[...], before_grad_ref[...], ((0,), (0,))).astype(BF16)
    second_ref[...] = dot(active_ref[...], out_grad_ref[...], ((0,), (0,))).astype(BF16)


def weight_grads(saved):
    tile = WG_TILE
    return pl.pallas_call(
        weight_grad_kernel,
        grid=(FF // tile,),
        in_specs=[
            pl.BlockSpec((LIVE, D), lambda n: (0, 0)),
            pl.BlockSpec((LIVE, tile), lambda n: (0, (2 * D + FF) // tile + n)),
            pl.BlockSpec((LIVE, tile), lambda n: (0, 2 * D // tile + n)),
            pl.BlockSpec((LIVE, D), lambda n: (0, 1)),
        ],
        out_specs=[
            pl.BlockSpec((D, tile), lambda n: (0, n)),
            pl.BlockSpec((tile, D), lambda n: (n, 0)),
        ],
        out_shape=[
            jax.ShapeDtypeStruct((D, FF), BF16),
            jax.ShapeDtypeStruct((FF, D), BF16),
        ],
        compiler_params=params(24),
        cost_estimate=pl.CostEstimate(
            flops=4 * LIVE * D * FF, bytes_accessed=11 * MB, transcendentals=0
        ),
    )(saved, saved, saved, saved)


def combine_kernel(
    rows_ref, index_ref, count_ref, resid_ref, upstream_ref, output_ref, grad_ref, stage, stage_g
):
    stage_rows(stage, rows_ref, 0)
    stage_rows(stage_g, rows_ref, 1)
    mixture = jnp.zeros((FR, D), F32)
    normed_grad = jnp.zeros((FR, D), F32)
    for slot in range(SLOT):
        spread = spread_matrix(index_ref, count_ref, slot).astype(BF16)
        mixture += dot(spread, unpack_rows(stage, slot).astype(BF16))
        normed_grad += dot(spread, unpack_rows(stage_g, slot).astype(BF16))
    resid = resid_ref[...].astype(F32)
    output_ref[...] = (resid + mixture).astype(BF16)
    unit, inverse = normalize(resid)
    first_mean = jnp.mean(normed_grad, axis=-1, keepdims=True)
    second_mean = jnp.mean(normed_grad * unit, axis=-1, keepdims=True)
    grad = inverse * (normed_grad - first_mean - unit * second_mean)
    grad_ref[...] = (upstream_ref[...].astype(F32) + grad).astype(BF16)


def combine(rows, index, count, resid, upstream):
    return pl.pallas_call(
        combine_kernel,
        out_shape=[jax.ShapeDtypeStruct((FR, D), BF16)] * 2,
        scratch_shapes=[pltpu.VMEM((DEVS * ROWS, 128), F32)] * 2,
        compiler_params=params(56),
        cost_estimate=pl.CostEstimate(
            flops=4 * DEVS * SLOT * FR * D, bytes_accessed=3 * MB, transcendentals=0
        ),
    )(rows, index, count, resid, upstream)


def exchange(rows, axes):
    return lax.all_to_all(rows, axes, split_axis=0, concat_axis=0, tiled=True)


def local(
    frames,
    cotangent,
    lengths,
    qkv_weight,
    out_weight,
    router,
    expert_in,
    expert_out,
    send_index,
    send_count,
):
    own_frames = frames[0]
    upstream = cotangent[0]
    index = jnp.transpose(send_index, (2, 0, 1))
    everywhere = ("seq", "exp")

    own = lax.axis_index("seq").astype(jnp.int32)
    scalars = jnp.concatenate([lengths, own[None]])

    parts = exchange(project(own_frames, index, send_count, qkv_weight), "seq")
    packed = gather_rows(upstream, own_frames, index, send_count)
    attended, packed = attend(scalars, parts, packed)
    arrived = exchange(packed, everywhere)
    pieces = [attended[0]]
    for step in range(1, HEADS):
        ring = [(source, (source + step) % HEADS) for source in range(HEADS)]
        pieces.append(lax.ppermute(attended[step], "seq", ring))
    resid = residual(scalars, pieces, own_frames, out_weight)
    back, grad_route, saved = expert(
        arrived, expert_in[0], expert_out[0], out_weight, router, resid
    )
    arrived_back = exchange(back, everywhere)
    grad_first, grad_second = weight_grads(saved)
    output, grad_resid = combine(arrived_back, index, send_count, resid, upstream)
    return (output[None], grad_resid[None], grad_first[None], grad_second[None], grad_route)


def solution(mesh):
    in_specs = (
        P("exp", "seq", None),
        P("exp", "seq", None),
        P("exp"),
        P(),
        P(),
        P(("seq", "exp"), None),
        P(("seq", "exp"), None, None),
        P(("seq", "exp"), None, None),
        P(("seq", "exp"), None, None),
        P(("seq", "exp"), None),
    )
    out_specs = (
        P("exp", "seq", None),
        P("exp", "seq", None),
        P(("seq", "exp"), None, None),
        P(("seq", "exp"), None, None),
        P(("seq", "exp"), None),
    )
    return jax.shard_map(local, mesh=mesh, in_specs=in_specs, out_specs=out_specs, check_vma=False)
```

```python
import jax
import jax.numpy as jnp
from jax import lax
from jax.experimental import pallas as pl
from jax.experimental.pallas import tpu as pltpu
from jax.sharding import PartitionSpec as P

HEADS = 8
HD = 64
D = 1024
FF = 2048
FR = 128
DEVS = 128
SLOT = 3
KEYS = 1024
LIVE = 256
TILES = D // 128
ROWS = SLOT * TILES

epsilon = 1e-05
masked_score = -1e30
empty_mark = 2.0**100
empty_bound = 2.0**99

F32 = jnp.float32
BF16 = jnp.bfloat16
MB = 1024 * 1024


def params(mib):
    return pltpu.CompilerParams(vmem_limit_bytes=mib * MB)


def whole(shape):
    return pl.BlockSpec(shape, lambda *_: (0,) * len(shape))


def dot(a, b, dims=((1,), (0,))):
    return lax.dot_general(a, b, (dims, ((), ())), preferred_element_type=F32)


def normalize(values):
    center = jnp.mean(values, axis=-1, keepdims=True)
    shifted = values - center
    spread = jnp.mean(jnp.square(shifted), axis=-1, keepdims=True)
    inverse = lax.rsqrt(spread + epsilon)
    return shifted * inverse, inverse


def spread_matrix(index_ref, count_ref, slot):
    frame = lax.broadcasted_iota(jnp.int32, (FR, DEVS), 0)
    named = jnp.broadcast_to(index_ref[slot], (FR, DEVS)) == frame
    used = jnp.broadcast_to(count_ref[...], (FR, DEVS)) > slot
    return jnp.where(named & used, 1.0, 0.0)


def pack_rows(stage, rows, slot):
    for tile in range(TILES):
        at = pl.ds(slot * TILES + tile, DEVS, stride=ROWS)
        stage[at, :] = rows[:, tile * 128 : (tile + 1) * 128]


def stage_rows(stage, rows_ref, half):
    stage[...] = rows_ref[:, half].astype(F32).reshape(DEVS * ROWS, 128)


def unpack_rows(stage, slot):
    tiles = [stage[pl.ds(slot * TILES + tile, DEVS, stride=ROWS), :] for tile in range(TILES)]
    return jnp.concatenate(tiles, axis=1)


PART = HD * 3
HALF = HEADS * HD


PROJECT_STEPS = 3


def project_kernel(frames_ref, weight_hbm, out_ref, weight_ref, sems):
    width = 3 * HALF // PROJECT_STEPS
    loads = []
    for step in range(PROJECT_STEPS):
        columns = pl.ds(step * width, width)
        loads.append(pltpu.make_async_copy(
            weight_hbm.at[:, columns], weight_ref.at[:, columns], sems.at[step]
        ))
        loads[-1].start()
    normed = normalize(frames_ref[...].astype(F32))[0].astype(BF16)
    for step in range(PROJECT_STEPS):
        loads[step].wait()
        block = dot(normed, weight_ref[:, pl.ds(step * width, width)]).astype(BF16).T
        for piece in range(width // HD):
            part, head = divmod(step * width // HD + piece, HEADS)
            start = head * PART + part * HD
            out_ref[start : start + HD, :] = block[piece * HD : (piece + 1) * HD]


def project(frames, weight):
    vmem = pl.BlockSpec(memory_space=pltpu.VMEM)
    return pl.pallas_call(
        project_kernel,
        in_specs=[vmem, pl.BlockSpec(memory_space=pl.ANY)],
        out_specs=vmem,
        out_shape=jax.ShapeDtypeStruct((HEADS * PART, FR), BF16),
        scratch_shapes=[
            pltpu.VMEM((D, 3 * HALF), BF16),
            pltpu.SemaphoreType.DMA((PROJECT_STEPS,)),
        ],
        compiler_params=params(56),
        cost_estimate=pl.CostEstimate(
            flops=2 * FR * D * 3 * HALF, bytes_accessed=4 * MB, transcendentals=0
        ),
    )(frames, weight)


def staged(stage):
    return stage[...].reshape(DEVS, 1, ROWS, 128).astype(BF16)


def gather_kernel(table_ref, index_ref, count_ref, out_ref, stage):
    count_column = jnp.broadcast_to(count_ref[...].astype(F32), (DEVS, DEVS)).T
    for slot in range(SLOT):
        pick = spread_matrix(index_ref, count_ref, slot).T.astype(BF16)
        rows = dot(pick, table_ref[...])
        mark = jnp.where(count_column[:, 0:1] > slot, 0.0, empty_mark)
        pack_rows(stage, rows + mark, slot)
    out_ref[...] = staged(stage)


def gather_rows(table, index, count):
    return pl.pallas_call(
        gather_kernel,
        grid=(1,),
        in_specs=[whole((FR, D)), whole((SLOT, 1, DEVS)), whole((1, DEVS))],
        out_specs=pl.BlockSpec((DEVS, 1, ROWS, 128), lambda n: (0, 1, 0, 0)),
        out_shape=jax.ShapeDtypeStruct((DEVS, 2, ROWS, 128), BF16),
        scratch_shapes=[pltpu.VMEM((DEVS * ROWS, 128), F32)],
        compiler_params=params(20),
        cost_estimate=pl.CostEstimate(
            flops=2 * DEVS * SLOT * FR * D, bytes_accessed=2 * MB, transcendentals=0
        ),
    )(table, index, count)


QUERIES = 1024


def attend_kernel(length_ref, parts_ref, out_ref):
    parts = [parts_ref[s * PART : (s + 1) * PART, :] for s in range(HEADS)]
    q = jnp.concatenate([part[:HD] for part in parts], axis=1)
    k = jnp.concatenate([part[HD : 2 * HD] for part in parts], axis=1).astype(F32)
    k = (k * HD ** (-0.5)).T.astype(BF16)
    v = jnp.concatenate([part[2 * HD :] for part in parts], axis=1)
    live = lax.broadcasted_iota(jnp.int32, (KEYS, QUERIES), 0) < length_ref[0]
    for first in range(0, KEYS, QUERIES):
        scores = dot(k, q[:, first : first + QUERIES])
        scores = jnp.where(live, scores, masked_score)
        top = jnp.max(scores, axis=0, keepdims=True)
        weights = jnp.exp(scores - top)
        total = jnp.sum(weights, axis=0, keepdims=True)
        mixed = (dot(v, weights.astype(BF16)) / total).astype(BF16)
        for piece in range(QUERIES // FR):
            source = first // FR + piece
            out_ref[source * HD : (source + 1) * HD, :] = mixed[:, piece * FR : (piece + 1) * FR]


def attend(length, parts):
    return pl.pallas_call(
        attend_kernel,
        in_specs=[
            pl.BlockSpec(memory_space=pltpu.SMEM),
            pl.BlockSpec(memory_space=pltpu.VMEM),
        ],
        out_shape=jax.ShapeDtypeStruct((HALF, FR), BF16),
        compiler_params=params(24),
        cost_estimate=pl.CostEstimate(
            flops=4 * KEYS * KEYS * HD, bytes_accessed=MB // 2, transcendentals=KEYS * KEYS
        ),
    )(length, parts)


def residual_kernel(
    attended_ref, frames_ref, weight_ref, index_ref, count_ref, packed_ref,
    resid_ref, out_ref, stage,
):
    attended = attended_ref[...].astype(F32).T.astype(BF16)
    resid = (frames_ref[...].astype(F32) + dot(attended, weight_ref[...])).astype(BF16)
    resid_ref[...] = resid
    mid = normalize(resid.astype(F32))[0].astype(BF16)
    picks = [spread_matrix(index_ref, count_ref, slot).T for slot in range(SLOT)]
    rows = dot(jnp.concatenate(picks, axis=0).astype(BF16), mid)
    for slot in range(SLOT):
        pack_rows(stage, rows[slot * DEVS : (slot + 1) * DEVS], slot)
    out_ref[...] = staged(stage)


def residual(attended, frames, weight, index, count, packed):
    return pl.pallas_call(
        residual_kernel,
        grid=(1,),
        in_specs=[
            whole((HALF, FR)),
            whole((FR, D)),
            whole((HALF, D)),
            whole((SLOT, 1, DEVS)),
            whole((1, DEVS)),
            pl.BlockSpec(memory_space=pl.ANY),
        ],
        out_specs=[
            whole((FR, D)),
            pl.BlockSpec((DEVS, 1, ROWS, 128), lambda n: (0, 0, 0, 0)),
        ],
        out_shape=[
            jax.ShapeDtypeStruct((FR, D), BF16),
            jax.ShapeDtypeStruct((DEVS, 2, ROWS, 128), BF16),
        ],
        input_output_aliases={5: 1},
        scratch_shapes=[pltpu.VMEM((DEVS * ROWS, 128), F32)],
        compiler_params=params(24),
        cost_estimate=pl.CostEstimate(
            flops=2 * FR * HALF * D + 2 * DEVS * SLOT * FR * D,
            bytes_accessed=3 * MB, transcendentals=0,
        ),
    )(attended, frames, weight, index, count, packed)


FF_TILE = 2048
FF_STEPS = FF // FF_TILE
WG_TILE = 512
gelu_scale = (2.0 / jnp.pi) ** 0.5
gelu_cubic = 0.044715


def seats(first_column):
    total = SLOT * DEVS
    live = first_column < empty_bound
    ahead = lax.broadcasted_iota(jnp.int32, (total, total), 0) >= lax.broadcasted_iota(
        jnp.int32, (total, total), 1
    )
    ranks = dot(jnp.where(ahead, 1.0, 0.0).astype(BF16), jnp.where(live, 1.0, 0.0).astype(BF16))
    seat = jnp.where(live, ranks - 1.0, -1.0)[:, 0:1].astype(jnp.int32)
    return jnp.where(seat == lax.broadcasted_iota(jnp.int32, (total, LIVE), 1), 1.0, 0.0)


def expert_kernel(
    rows_ref, first_hbm, second_hbm, router_ref,
    back_ref, route_grad_ref, saved_ref,
    stage_x, stage_g, pulled_ref, first_ref, second_ref, first_sem, second_sem,
):
    picked_ref = saved_ref.at[:, :D]
    out_grad_ref = saved_ref.at[:, D : 2 * D]
    active_ref = saved_ref.at[:, 2 * D : 2 * D + FF]
    before_grad_ref = saved_ref.at[:, 2 * D + FF :]

    def tiles(step):
        return pl.ds(step * FF_TILE, FF_TILE)

    first_loads, second_loads = [], []
    for step in range(FF_STEPS):
        columns = tiles(step)
        first_loads.append(pltpu.make_async_copy(
            first_hbm.at[:, columns], first_ref.at[:, columns], first_sem.at[step]
        ))
        second_loads.append(pltpu.make_async_copy(
            second_hbm.at[columns, :], second_ref.at[columns, :], second_sem.at[step]
        ))
        second_loads[-1].start()
        first_loads[-1].start()

    stage_rows(stage_g, rows_ref, 1)
    grads = jnp.concatenate([unpack_rows(stage_g, slot) for slot in range(SLOT)], axis=0)
    place = seats(grads[:, 0:128])
    take = place.T.astype(BF16)
    place = place.astype(BF16)
    stage_rows(stage_x, rows_ref, 0)
    rows = [unpack_rows(stage_x, slot) for slot in range(SLOT)]
    both = jnp.concatenate([grads, jnp.concatenate(rows, axis=0)], axis=1)
    both = dot(take, both.astype(BF16))
    grads = both[:, :D].astype(BF16)
    picked_wide = both[:, D:]
    for step in range(FF_STEPS):
        second_loads[step].wait()
        pulled_ref[:, tiles(step)] = dot(grads, second_ref[tiles(step), :], ((1,), (1,)))
    picked = picked_wide.astype(BF16)
    picked_ref[...] = picked
    logits = jnp.sum(picked_wide * router_ref[...], axis=-1, keepdims=True)
    gate = 1.0 / (1.0 + jnp.exp(-logits))
    out_grad_ref[...] = (gate * grads.astype(F32)).astype(BF16)

    logit = jnp.zeros((LIVE, 1), F32)
    for step in range(FF_STEPS):
        columns = tiles(step)
        pulled = pulled_ref[:, columns]
        first_loads[step].wait()
        before = dot(picked, first_ref[:, columns])
        square = before * before
        bend = jnp.tanh(before * (gelu_scale + (gelu_scale * gelu_cubic) * square))
        half = 0.5 + 0.5 * bend
        active = (before * half).astype(BF16)
        slope = half + (before * (1.0 - bend * bend)) * (
            0.5 * gelu_scale + (1.5 * gelu_scale * gelu_cubic) * square
        )
        active_ref[:, columns] = active
        before_grad_ref[:, columns] = (gate * pulled * slope).astype(BF16)
        logit += jnp.sum(active.astype(F32) * pulled, axis=-1, keepdims=True)

    logit_grad = logit * gate * (1.0 - gate)
    route_grad_ref[...] = jnp.sum(logit_grad * picked_ref[...].astype(F32), axis=0, keepdims=True)
    returned = (gate * dot(active_ref[...], second_ref[...])).astype(BF16)
    row_grad = dot(before_grad_ref[...], first_ref[...], ((1,), (1,)))
    row_grad = (row_grad + logit_grad * router_ref[...]).astype(BF16)
    back = dot(place, jnp.concatenate([returned, row_grad], axis=1))
    for slot in range(SLOT):
        sources = slice(slot * DEVS, (slot + 1) * DEVS)
        pack_rows(stage_x, back[sources, :D], slot)
        pack_rows(stage_g, back[sources, D:], slot)
    back_ref[:, 0:1] = staged(stage_x)
    back_ref[:, 1:2] = staged(stage_g)


def expert(rows, first, second, router):
    vmem = pl.BlockSpec(memory_space=pltpu.VMEM)
    hbm = pl.BlockSpec(memory_space=pl.ANY)
    return pl.pallas_call(
        expert_kernel,
        in_specs=[vmem, hbm, hbm, vmem],
        out_specs=[vmem, vmem, vmem],
        out_shape=[
            jax.ShapeDtypeStruct((DEVS, 2, ROWS, 128), BF16),
            jax.ShapeDtypeStruct((1, D), F32),
            jax.ShapeDtypeStruct((LIVE, 2 * D + 2 * FF), BF16),
        ],
        scratch_shapes=[
            pltpu.VMEM((DEVS * ROWS, 128), F32),
            pltpu.VMEM((DEVS * ROWS, 128), F32),
            pltpu.VMEM((LIVE, FF), F32),
            pltpu.VMEM((D, FF), BF16),
            pltpu.VMEM((FF, D), BF16),
            pltpu.SemaphoreType.DMA((FF_STEPS,)),
            pltpu.SemaphoreType.DMA((FF_STEPS,)),
        ],
        compiler_params=params(44),
        cost_estimate=pl.CostEstimate(
            flops=8 * LIVE * D * FF, bytes_accessed=14 * MB, transcendentals=LIVE * FF
        ),
    )(rows, first, second, router)


def weight_grad_kernel(picked_ref, before_grad_ref, active_ref, out_grad_ref, first_ref, second_ref):
    first_ref[...] = dot(picked_ref[...], before_grad_ref[...], ((0,), (0,))).astype(BF16)
    second_ref[...] = dot(active_ref[...], out_grad_ref[...], ((0,), (0,))).astype(BF16)


def weight_grads(saved):
    tile = WG_TILE
    return pl.pallas_call(
        weight_grad_kernel,
        grid=(FF // tile,),
        in_specs=[
            pl.BlockSpec((LIVE, D), lambda n: (0, 0)),
            pl.BlockSpec((LIVE, tile), lambda n: (0, (2 * D + FF) // tile + n)),
            pl.BlockSpec((LIVE, tile), lambda n: (0, 2 * D // tile + n)),
            pl.BlockSpec((LIVE, D), lambda n: (0, 1)),
        ],
        out_specs=[
            pl.BlockSpec((D, tile), lambda n: (0, n)),
            pl.BlockSpec((tile, D), lambda n: (n, 0)),
        ],
        out_shape=[
            jax.ShapeDtypeStruct((D, FF), BF16),
            jax.ShapeDtypeStruct((FF, D), BF16),
        ],
        compiler_params=params(24),
        cost_estimate=pl.CostEstimate(
            flops=4 * LIVE * D * FF, bytes_accessed=11 * MB, transcendentals=0
        ),
    )(saved, saved, saved, saved)


def combine_kernel(
    rows_ref, index_ref, count_ref, resid_ref, upstream_ref, output_ref, grad_ref, stage, stage_g
):
    stage_rows(stage, rows_ref, 0)
    stage_rows(stage_g, rows_ref, 1)
    spreads = [spread_matrix(index_ref, count_ref, slot).astype(BF16) for slot in range(SLOT)]
    rows = [
        jnp.concatenate([unpack_rows(stage, slot), unpack_rows(stage_g, slot)], axis=1)
        for slot in range(SLOT)
    ]
    sums = dot(jnp.concatenate(spreads, axis=1), jnp.concatenate(rows, axis=0).astype(BF16))
    mixture = sums[:, :D]
    normed_grad = sums[:, D:]
    resid = resid_ref[...].astype(F32)
    output_ref[...] = (resid + mixture).astype(BF16)
    unit, inverse = normalize(resid)
    first_mean = jnp.mean(normed_grad, axis=-1, keepdims=True)
    second_mean = jnp.mean(normed_grad * unit, axis=-1, keepdims=True)
    grad = inverse * (normed_grad - first_mean - unit * second_mean)
    grad_ref[...] = (upstream_ref[...].astype(F32) + grad).astype(BF16)


def combine(rows, index, count, resid, upstream):
    return pl.pallas_call(
        combine_kernel,
        out_shape=[jax.ShapeDtypeStruct((FR, D), BF16)] * 2,
        scratch_shapes=[pltpu.VMEM((DEVS * ROWS, 128), F32)] * 2,
        compiler_params=params(56),
        cost_estimate=pl.CostEstimate(
            flops=4 * DEVS * SLOT * FR * D, bytes_accessed=3 * MB, transcendentals=0
        ),
    )(rows, index, count, resid, upstream)


def exchange(rows, axes):
    return lax.all_to_all(rows, axes, split_axis=0, concat_axis=0, tiled=True)


def local(
    frames,
    cotangent,
    lengths,
    qkv_weight,
    out_weight,
    router,
    expert_in,
    expert_out,
    send_index,
    send_count,
):
    own_frames = frames[0]
    upstream = cotangent[0]
    index = jnp.transpose(send_index, (2, 0, 1))
    everywhere = ("seq", "exp")

    parts = project(own_frames, qkv_weight).reshape(HEADS, PART, FR)
    parts = exchange(parts, "seq").reshape(HEADS * PART, FR)
    packed = gather_rows(upstream, index, send_count)
    attended = attend(lengths, parts).reshape(HEADS, HD, FR)
    attended = exchange(attended, "seq").reshape(HALF, FR)
    resid, packed = residual(attended, own_frames, out_weight, index, send_count, packed)
    arrived = exchange(packed, everywhere)
    back, grad_route, saved = expert(
        arrived, expert_in[0], expert_out[0], router
    )
    arrived_back = exchange(back, everywhere)
    grad_first, grad_second = weight_grads(saved)
    output, grad_resid = combine(arrived_back, index, send_count, resid, upstream)
    return (output[None], grad_resid[None], grad_first[None], grad_second[None], grad_route)


def solution(mesh):
    in_specs = (
        P("exp", "seq", None),
        P("exp", "seq", None),
        P("exp"),
        P(),
        P(),
        P(("seq", "exp"), None),
        P(("seq", "exp"), None, None),
        P(("seq", "exp"), None, None),
        P(("seq", "exp"), None, None),
        P(("seq", "exp"), None),
    )
    out_specs = (
        P("exp", "seq", None),
        P("exp", "seq", None),
        P(("seq", "exp"), None, None),
        P(("seq", "exp"), None, None),
        P(("seq", "exp"), None),
    )
    return jax.shard_map(local, mesh=mesh, in_specs=in_specs, out_specs=out_specs, check_vma=False)
```

```python
import jax
import jax.numpy as jnp
from jax import lax
from jax.experimental import pallas as pl
from jax.experimental.pallas import tpu as pltpu
from jax.sharding import PartitionSpec as P

HEADS = 8
HD = 64
D = 1024
FF = 2048
FR = 128
DEVS = 128
SLOT = 3
KEYS = 1024
LIVE = 256
TILES = D // 128
ROWS = SLOT * TILES

epsilon = 1e-05
masked_score = -1e30
empty_mark = 2.0**100
empty_bound = 2.0**99

F32 = jnp.float32
BF16 = jnp.bfloat16
MB = 1024 * 1024


def params(mib):
    return pltpu.CompilerParams(vmem_limit_bytes=mib * MB)


def whole(shape):
    return pl.BlockSpec(shape, lambda *_: (0,) * len(shape))


def dot(a, b, dims=((1,), (0,))):
    return lax.dot_general(a, b, (dims, ((), ())), preferred_element_type=F32)


def normalize(values):
    center = jnp.mean(values, axis=-1, keepdims=True)
    shifted = values - center
    spread = jnp.mean(jnp.square(shifted), axis=-1, keepdims=True)
    inverse = lax.rsqrt(spread + epsilon)
    return shifted * inverse, inverse


def spread_matrix(index_ref, count_ref, slot):
    frame = lax.broadcasted_iota(jnp.int32, (FR, DEVS), 0)
    named = jnp.broadcast_to(index_ref[slot], (FR, DEVS)) == frame
    used = jnp.broadcast_to(count_ref[...], (FR, DEVS)) > slot
    return jnp.where(named & used, 1.0, 0.0)


def pack_rows(stage, rows, slot):
    for tile in range(TILES):
        at = pl.ds(slot * TILES + tile, DEVS, stride=ROWS)
        stage[at, :] = rows[:, tile * 128 : (tile + 1) * 128]


def stage_rows(stage, rows_ref, half):
    stage[...] = rows_ref[:, half].astype(F32).reshape(DEVS * ROWS, 128)


def unpack_rows(stage, slot):
    tiles = [stage[pl.ds(slot * TILES + tile, DEVS, stride=ROWS), :] for tile in range(TILES)]
    return jnp.concatenate(tiles, axis=1)


PART = HD * 3
HALF = HEADS * HD


PROJECT_STEPS = 3


def project_kernel(frames_ref, weight_hbm, out_ref, weight_ref, sems):
    width = 3 * HALF // PROJECT_STEPS
    loads = []
    for step in range(PROJECT_STEPS):
        columns = pl.ds(step * width, width)
        loads.append(pltpu.make_async_copy(
            weight_hbm.at[:, columns], weight_ref.at[:, columns], sems.at[step]
        ))
        loads[-1].start()
    normed = normalize(frames_ref[...].astype(F32))[0].astype(BF16)
    for step in range(PROJECT_STEPS):
        loads[step].wait()
        block = dot(normed, weight_ref[:, pl.ds(step * width, width)]).astype(BF16).T
        for piece in range(width // HD):
            part, head = divmod(step * width // HD + piece, HEADS)
            start = head * PART + part * HD
            out_ref[start : start + HD, :] = block[piece * HD : (piece + 1) * HD]


def project(frames, weight):
    vmem = pl.BlockSpec(memory_space=pltpu.VMEM)
    return pl.pallas_call(
        project_kernel,
        in_specs=[vmem, pl.BlockSpec(memory_space=pl.ANY)],
        out_specs=vmem,
        out_shape=jax.ShapeDtypeStruct((HEADS * PART, FR), BF16),
        scratch_shapes=[
            pltpu.VMEM((D, 3 * HALF), BF16),
            pltpu.SemaphoreType.DMA((PROJECT_STEPS,)),
        ],
        compiler_params=params(56),
        cost_estimate=pl.CostEstimate(
            flops=2 * FR * D * 3 * HALF, bytes_accessed=4 * MB, transcendentals=0
        ),
    )(frames, weight)


def staged(stage):
    return stage[...].reshape(DEVS, 1, ROWS, 128).astype(BF16)


def gather_kernel(table_ref, index_ref, count_ref, out_ref, stage):
    count_column = jnp.broadcast_to(count_ref[...].astype(F32), (DEVS, DEVS)).T
    for slot in range(SLOT):
        pick = spread_matrix(index_ref, count_ref, slot).T.astype(BF16)
        rows = dot(pick, table_ref[...])
        mark = jnp.where(count_column[:, 0:1] > slot, 0.0, empty_mark)
        pack_rows(stage, rows + mark, slot)
    out_ref[...] = staged(stage)


def gather_rows(table, index, count):
    return pl.pallas_call(
        gather_kernel,
        grid=(1,),
        in_specs=[whole((FR, D)), whole((SLOT, 1, DEVS)), whole((1, DEVS))],
        out_specs=pl.BlockSpec((DEVS, 1, ROWS, 128), lambda n: (0, 1, 0, 0)),
        out_shape=jax.ShapeDtypeStruct((DEVS, 2, ROWS, 128), BF16),
        scratch_shapes=[pltpu.VMEM((DEVS * ROWS, 128), F32)],
        compiler_params=params(20),
        cost_estimate=pl.CostEstimate(
            flops=2 * DEVS * SLOT * FR * D, bytes_accessed=2 * MB, transcendentals=0
        ),
    )(table, index, count)


QUERIES = 1024


def attend_kernel(length_ref, parts_ref, out_ref):
    parts = [parts_ref[s * PART : (s + 1) * PART, :] for s in range(HEADS)]
    q = jnp.concatenate([part[:HD] for part in parts], axis=1)
    k = jnp.concatenate([part[HD : 2 * HD] for part in parts], axis=1).astype(F32)
    k = (k * HD ** (-0.5)).T.astype(BF16)
    v = jnp.concatenate([part[2 * HD :] for part in parts], axis=1)
    live = lax.broadcasted_iota(jnp.int32, (KEYS, QUERIES), 0) < length_ref[0]
    for first in range(0, KEYS, QUERIES):
        scores = dot(k, q[:, first : first + QUERIES])
        scores = jnp.where(live, scores, masked_score)
        top = jnp.max(scores, axis=0, keepdims=True)
        weights = jnp.exp(scores - top)
        total = jnp.sum(weights, axis=0, keepdims=True)
        mixed = (dot(v, weights.astype(BF16)) / total).astype(BF16)
        for piece in range(QUERIES // FR):
            source = first // FR + piece
            out_ref[source * HD : (source + 1) * HD, :] = mixed[:, piece * FR : (piece + 1) * FR]


def attend(length, parts):
    return pl.pallas_call(
        attend_kernel,
        in_specs=[
            pl.BlockSpec(memory_space=pltpu.SMEM),
            pl.BlockSpec(memory_space=pltpu.VMEM),
        ],
        out_shape=jax.ShapeDtypeStruct((HALF, FR), BF16),
        compiler_params=params(24),
        cost_estimate=pl.CostEstimate(
            flops=4 * KEYS * KEYS * HD, bytes_accessed=MB // 2, transcendentals=KEYS * KEYS
        ),
    )(length, parts)


def residual_kernel(
    attended_ref, frames_ref, weight_ref, index_ref, count_ref, packed_ref,
    resid_ref, out_ref, stage,
):
    attended = attended_ref[...].astype(F32).T.astype(BF16)
    resid = (frames_ref[...].astype(F32) + dot(attended, weight_ref[...])).astype(BF16)
    resid_ref[...] = resid
    mid = normalize(resid.astype(F32))[0].astype(BF16)
    picks = [spread_matrix(index_ref, count_ref, slot).T for slot in range(SLOT)]
    rows = dot(jnp.concatenate(picks, axis=0).astype(BF16), mid)
    for slot in range(SLOT):
        pack_rows(stage, rows[slot * DEVS : (slot + 1) * DEVS], slot)
    out_ref[...] = staged(stage)


def residual(attended, frames, weight, index, count, packed):
    return pl.pallas_call(
        residual_kernel,
        grid=(1,),
        in_specs=[
            whole((HALF, FR)),
            whole((FR, D)),
            whole((HALF, D)),
            whole((SLOT, 1, DEVS)),
            whole((1, DEVS)),
            pl.BlockSpec(memory_space=pl.ANY),
        ],
        out_specs=[
            whole((FR, D)),
            pl.BlockSpec((DEVS, 1, ROWS, 128), lambda n: (0, 0, 0, 0)),
        ],
        out_shape=[
            jax.ShapeDtypeStruct((FR, D), BF16),
            jax.ShapeDtypeStruct((DEVS, 2, ROWS, 128), BF16),
        ],
        input_output_aliases={5: 1},
        scratch_shapes=[pltpu.VMEM((DEVS * ROWS, 128), F32)],
        compiler_params=params(24),
        cost_estimate=pl.CostEstimate(
            flops=2 * FR * HALF * D + 2 * DEVS * SLOT * FR * D,
            bytes_accessed=3 * MB, transcendentals=0,
        ),
    )(attended, frames, weight, index, count, packed)


FF_TILE = 1024
FF_STEPS = FF // FF_TILE
WG_TILE = 512
gelu_scale = (2.0 / jnp.pi) ** 0.5
gelu_cubic = 0.044715


def seats(first_column):
    total = SLOT * DEVS
    live = first_column < empty_bound
    ahead = lax.broadcasted_iota(jnp.int32, (total, total), 0) >= lax.broadcasted_iota(
        jnp.int32, (total, total), 1
    )
    ranks = dot(jnp.where(ahead, 1.0, 0.0).astype(BF16), jnp.where(live, 1.0, 0.0).astype(BF16))
    seat = jnp.where(live, ranks - 1.0, -1.0)[:, 0:1].astype(jnp.int32)
    return jnp.where(seat == lax.broadcasted_iota(jnp.int32, (total, LIVE), 1), 1.0, 0.0)


def expert_kernel(
    rows_ref, first_hbm, second_hbm, router_ref,
    back_ref, route_grad_ref, saved_ref,
    stage_x, stage_g, pulled_ref, first_ref, second_ref, first_sem, second_sem,
):
    picked_ref = saved_ref.at[:, :D]
    out_grad_ref = saved_ref.at[:, D : 2 * D]
    active_ref = saved_ref.at[:, 2 * D : 2 * D + FF]
    before_grad_ref = saved_ref.at[:, 2 * D + FF :]

    def tiles(step):
        return pl.ds(step * FF_TILE, FF_TILE)

    first_loads, second_loads = [], []
    for step in range(FF_STEPS):
        columns = tiles(step)
        first_loads.append(pltpu.make_async_copy(
            first_hbm.at[:, columns], first_ref.at[:, columns], first_sem.at[step]
        ))
        second_loads.append(pltpu.make_async_copy(
            second_hbm.at[columns, :], second_ref.at[columns, :], second_sem.at[step]
        ))
        second_loads[-1].start()
        first_loads[-1].start()

    stage_rows(stage_g, rows_ref, 1)
    grads = jnp.concatenate([unpack_rows(stage_g, slot) for slot in range(SLOT)], axis=0)
    place = seats(grads[:, 0:128])
    take = place.T.astype(BF16)
    place = place.astype(BF16)
    grads = dot(take, grads.astype(BF16)).astype(BF16)
    for step in range(FF_STEPS):
        second_loads[step].wait()
        pulled_ref[:, tiles(step)] = dot(grads, second_ref[tiles(step), :], ((1,), (1,)))
    stage_rows(stage_x, rows_ref, 0)
    rows = [unpack_rows(stage_x, slot).astype(BF16) for slot in range(SLOT)]
    picked_wide = dot(take, jnp.concatenate(rows, axis=0))
    picked = picked_wide.astype(BF16)
    picked_ref[...] = picked
    logits = jnp.sum(picked_wide * router_ref[...], axis=-1, keepdims=True)
    gate = 1.0 / (1.0 + jnp.exp(-logits))
    out_grad_ref[...] = (gate * grads.astype(F32)).astype(BF16)

    logit = jnp.zeros((LIVE, 1), F32)
    for step in range(FF_STEPS):
        columns = tiles(step)
        pulled = pulled_ref[:, columns]
        first_loads[step].wait()
        before = dot(picked, first_ref[:, columns])
        square = before * before
        bend = jnp.tanh(before * (gelu_scale + (gelu_scale * gelu_cubic) * square))
        half = 0.5 + 0.5 * bend
        active = (before * half).astype(BF16)
        slope = half + (before * (1.0 - bend * bend)) * (
            0.5 * gelu_scale + (1.5 * gelu_scale * gelu_cubic) * square
        )
        active_ref[:, columns] = active
        before_grad_ref[:, columns] = (gate * pulled * slope).astype(BF16)
        logit += jnp.sum(active.astype(F32) * pulled, axis=-1, keepdims=True)

    logit_grad = logit * gate * (1.0 - gate)
    route_grad_ref[...] = jnp.sum(logit_grad * picked_ref[...].astype(F32), axis=0, keepdims=True)
    returned = (gate * dot(active_ref[...], second_ref[...])).astype(BF16)
    row_grad = dot(before_grad_ref[...], first_ref[...], ((1,), (1,)))
    row_grad = (row_grad + logit_grad * router_ref[...]).astype(BF16)
    back = dot(place, jnp.concatenate([returned, row_grad], axis=1))
    for slot in range(SLOT):
        sources = slice(slot * DEVS, (slot + 1) * DEVS)
        pack_rows(stage_x, back[sources, :D], slot)
        pack_rows(stage_g, back[sources, D:], slot)
    back_ref[:, 0:1] = staged(stage_x)
    back_ref[:, 1:2] = staged(stage_g)


def expert(rows, first, second, router):
    vmem = pl.BlockSpec(memory_space=pltpu.VMEM)
    hbm = pl.BlockSpec(memory_space=pl.ANY)
    return pl.pallas_call(
        expert_kernel,
        in_specs=[vmem, hbm, hbm, vmem],
        out_specs=[vmem, vmem, vmem],
        out_shape=[
            jax.ShapeDtypeStruct((DEVS, 2, ROWS, 128), BF16),
            jax.ShapeDtypeStruct((1, D), F32),
            jax.ShapeDtypeStruct((LIVE, 2 * D + 2 * FF), BF16),
        ],
        scratch_shapes=[
            pltpu.VMEM((DEVS * ROWS, 128), F32),
            pltpu.VMEM((DEVS * ROWS, 128), F32),
            pltpu.VMEM((LIVE, FF), F32),
            pltpu.VMEM((D, FF), BF16),
            pltpu.VMEM((FF, D), BF16),
            pltpu.SemaphoreType.DMA((FF_STEPS,)),
            pltpu.SemaphoreType.DMA((FF_STEPS,)),
        ],
        compiler_params=params(44),
        cost_estimate=pl.CostEstimate(
            flops=8 * LIVE * D * FF, bytes_accessed=14 * MB, transcendentals=LIVE * FF
        ),
    )(rows, first, second, router)


def weight_grad_kernel(picked_ref, before_grad_ref, active_ref, out_grad_ref, first_ref, second_ref):
    first_ref[...] = dot(picked_ref[...], before_grad_ref[...], ((0,), (0,))).astype(BF16)
    second_ref[...] = dot(active_ref[...], out_grad_ref[...], ((0,), (0,))).astype(BF16)


def weight_grads(saved):
    tile = WG_TILE
    return pl.pallas_call(
        weight_grad_kernel,
        grid=(FF // tile,),
        in_specs=[
            pl.BlockSpec((LIVE, D), lambda n: (0, 0)),
            pl.BlockSpec((LIVE, tile), lambda n: (0, (2 * D + FF) // tile + n)),
            pl.BlockSpec((LIVE, tile), lambda n: (0, 2 * D // tile + n)),
            pl.BlockSpec((LIVE, D), lambda n: (0, 1)),
        ],
        out_specs=[
            pl.BlockSpec((D, tile), lambda n: (0, n)),
            pl.BlockSpec((tile, D), lambda n: (n, 0)),
        ],
        out_shape=[
            jax.ShapeDtypeStruct((D, FF), BF16),
            jax.ShapeDtypeStruct((FF, D), BF16),
        ],
        compiler_params=params(24),
        cost_estimate=pl.CostEstimate(
            flops=4 * LIVE * D * FF, bytes_accessed=11 * MB, transcendentals=0
        ),
    )(saved, saved, saved, saved)


def combine_kernel(
    rows_ref, index_ref, count_ref, resid_ref, upstream_ref, output_ref, grad_ref, stage, stage_g
):
    stage_rows(stage, rows_ref, 0)
    stage_rows(stage_g, rows_ref, 1)
    spreads = [spread_matrix(index_ref, count_ref, slot).astype(BF16) for slot in range(SLOT)]
    rows = [
        jnp.concatenate([unpack_rows(stage, slot), unpack_rows(stage_g, slot)], axis=1)
        for slot in range(SLOT)
    ]
    sums = dot(jnp.concatenate(spreads, axis=1), jnp.concatenate(rows, axis=0).astype(BF16))
    mixture = sums[:, :D]
    normed_grad = sums[:, D:]
    resid = resid_ref[...].astype(F32)
    output_ref[...] = (resid + mixture).astype(BF16)
    unit, inverse = normalize(resid)
    first_mean = jnp.mean(normed_grad, axis=-1, keepdims=True)
    second_mean = jnp.mean(normed_grad * unit, axis=-1, keepdims=True)
    grad = inverse * (normed_grad - first_mean - unit * second_mean)
    grad_ref[...] = (upstream_ref[...].astype(F32) + grad).astype(BF16)


def combine(rows, index, count, resid, upstream):
    return pl.pallas_call(
        combine_kernel,
        out_shape=[jax.ShapeDtypeStruct((FR, D), BF16)] * 2,
        scratch_shapes=[pltpu.VMEM((DEVS * ROWS, 128), F32)] * 2,
        compiler_params=params(56),
        cost_estimate=pl.CostEstimate(
            flops=4 * DEVS * SLOT * FR * D, bytes_accessed=3 * MB, transcendentals=0
        ),
    )(rows, index, count, resid, upstream)


def exchange(rows, axes):
    return lax.all_to_all(rows, axes, split_axis=0, concat_axis=0, tiled=True)


def local(
    frames,
    cotangent,
    lengths,
    qkv_weight,
    out_weight,
    router,
    expert_in,
    expert_out,
    send_index,
    send_count,
):
    own_frames = frames[0]
    upstream = cotangent[0]
    index = jnp.transpose(send_index, (2, 0, 1))
    everywhere = ("seq", "exp")

    parts = project(own_frames, qkv_weight).reshape(HEADS, PART, FR)
    parts = exchange(parts, "seq").reshape(HEADS * PART, FR)
    packed = gather_rows(upstream, index, send_count)
    attended = attend(lengths, parts).reshape(HEADS, HD, FR)
    attended = exchange(attended, "seq").reshape(HALF, FR)
    resid, packed = residual(attended, own_frames, out_weight, index, send_count, packed)
    arrived = exchange(packed, everywhere)
    back, grad_route, saved = expert(
        arrived, expert_in[0], expert_out[0], router
    )
    arrived_back = exchange(back, everywhere)
    grad_first, grad_second = weight_grads(saved)
    output, grad_resid = combine(arrived_back, index, send_count, resid, upstream)
    return (output[None], grad_resid[None], grad_first[None], grad_second[None], grad_route)


def solution(mesh):
    in_specs = (
        P("exp", "seq", None),
        P("exp", "seq", None),
        P("exp"),
        P(),
        P(),
        P(("seq", "exp"), None),
        P(("seq", "exp"), None, None),
        P(("seq", "exp"), None, None),
        P(("seq", "exp"), None, None),
        P(("seq", "exp"), None),
    )
    out_specs = (
        P("exp", "seq", None),
        P("exp", "seq", None),
        P(("seq", "exp"), None, None),
        P(("seq", "exp"), None, None),
        P(("seq", "exp"), None),
    )
    return jax.shard_map(local, mesh=mesh, in_specs=in_specs, out_specs=out_specs, check_vma=False)
```
